32 devices in a mesh: stn: 4 (over z), chan: 8 (over y, x, core).
Axes of the slice: x: 2, y: 2, z: 4, core: 2. Of those that a mesh axis runs over, the one named last changes fastest.
Arguments:
- voltages: bfloat16 [256, 128, 512], P('stn', 'chan'), may hold values from -6 to 6
- block_facet: int32 [8, 4, 2048, 1], P('chan', 'stn'), may hold values from 0 to 3; in each aligned block of 2048 rows (0 to 2047, 2048 to 4095, ..., all dimensions but the last counted through in order) at most 768 rows name the same one
- block_tile: int32 [8, 4, 2048], P('chan', 'stn'), may hold values from 0 to 15
- vis_offset: int32 [8, 4, 2048, 128], P('chan', 'stn'), may hold values from 0 to 624
- kernel_taps: bfloat16 [2, 8], replicated, may hold values from 0.19921875 to 1
Outputs:
- image: float32 [2, 512, 128], P(None, ('stn', 'chan'))
The draws below stay inside these ranges and needn't reach their ends.
Inputs may be any that keep to these rules, and one draw needn't show every extreme that they name: `block_facet`: among the blocks of one device (one index of the first two dimensions) at most 768 name one facet; in every draw some facet is named by exactly 768 of some device's blocks.
All inputs are finite; a program needn't handle non-finite values.
Results may differ from the reference program's by a relative error of at most 0.0041.
Values may be sent and summed in bfloat16 or wider, within the bound.
No kernel may reach another device: no remote copies, remote signals or barrier semaphores. Data moves between devices by JAX's collectives and lax.ppermute only.
A program may use at most 64 MiB of HBM per device.

```python
import math
import jax
import jax.numpy as jnp
import numpy as np
from jax import lax

STATIONS = 256
SAMPLES = 256
VB = 128
TILE = 32
KT = 8
TS = 4
FACETS = 4
CGROUPS = 8
CHANNELS = 128
BLK_DEV = 2048
CAP = 768
TT = 16
FG = 128
OFFS = 25


def with_ends(entries, rng, least, high):
    place = [jax.random.randint(jax.random.fold_in(rng, axis), (), 0, length) for axis, length in enumerate(entries.shape)]
    main_axis = entries.shape.index(max(entries.shape))
    neighbour = place[:main_axis] + [(place[main_axis] + 1) % entries.shape[main_axis]] + place[main_axis + 1:]
    return entries.at[tuple(place)].set(least).at[tuple(neighbour)].set(high)


def shard_levels(own_key, extent, shards, smallest, top_value):
    loudness = 1.0
    for dim, parts in shards:
        heights = jax.random.uniform(jax.random.fold_in(jax.random.fold_in(own_key, 6), dim), (parts,), jnp.float32, smallest / len(shards), top_value / len(shards))
        loudness = loudness * jnp.repeat(jnp.exp(heights), extent[dim] // parts).reshape((-1,) + (1,) * (len(extent) - 1 - dim))
    return loudness


def deal_out(key, own, number, rows, count, top, most, skew):
    ranking = jax.random.permutation(key, count)
    packed, usual = shares(count, rows * top, most, skew, True), shares(count, rows * top, most, skew, False)
    places = jnp.arange(count)

    def named(tallies, rotation):
        used = int((tallies > 0).sum())
        fixed = max(1, used // 4)
        moved = fixed + (places - fixed + rotation * (used - fixed)) % max(1, count - fixed)
        return jnp.zeros((count,), jnp.int32).at[ranking[jnp.where(places < fixed, places, moved)]].set(jnp.asarray(tallies, jnp.int32))

    tallies = jnp.where(number % 4 == 0, named(packed, number // 4), named(usual, number - number // 4 - 1))
    mixed = jax.random.permutation(jax.random.fold_in(own, 3), count)
    source_of, receiver = mixed[0:count // 2 * 2:2], mixed[1:count // 2 * 2:2]
    margin = jnp.minimum(tallies[source_of] - 1, most - tallies[receiver]) // 2
    margin = jnp.where((source_of == ranking[0]) | (receiver == ranking[0]) | (tallies[receiver] == 0), 0, jnp.maximum(margin, 0))
    moved = jax.random.randint(jax.random.fold_in(own, 4), (count // 2,), 0, 1 << 20) % (margin + 1)
    tallies = tallies.at[source_of].add(-moved).at[receiver].add(moved)
    items = jnp.searchsorted(jnp.cumsum(tallies), jnp.arange(rows * top), side="right").astype(jnp.int32)
    grid = items.reshape(top, rows).T
    grid = grid[jax.random.permutation(jax.random.fold_in(own, 1), rows)]
    rotation = jax.random.randint(jax.random.fold_in(own, 2), (rows, 1), 0, top)
    return jnp.take_along_axis(grid, (jnp.arange(top)[None, :] + rotation) % top, axis=1)


def shares(count, total, reach, slope, full):
    weights = [(1 << 20) // math.isqrt(standing ** slope) + 1 for standing in range(1, count + 1)]
    largest = reach if full else min(reach, max(-(-total // count), total * weights[0] // sum(weights)))
    least = 1 if total - largest >= count - 1 else 0
    given, rest = [largest] + [least] * (count - 1), total - largest - least * (count - 1)
    while rest > 0:
        candidates = [i for i in range(1, count) if given[i] < largest] or [i for i in range(1, count) if given[i] < reach]
        pool, left = sum([weights[i] for i in candidates]), rest
        for i in candidates:
            more = min(reach - given[i], max(1, left * weights[i] // pool), rest)
            given[i] = given[i] + more
            rest = rest - more
    return np.array(given)


def normal_values(stream_key, dims, scale, most, split=(), held_as=jnp.bfloat16):
    values = scale * jax.random.normal(stream_key, dims, jnp.float32)
    if split:
        values = values * shard_levels(stream_key, dims, split, -0.22, 0.18)
    return jnp.clip(values, -most, most).astype(held_as)


def setup_inputs(seed: int = 0) -> dict:
    key_of = jax.random.split(jax.random.key(seed), 6)
    voltages = normal_values(key_of[0], (STATIONS, CHANNELS, 2 * SAMPLES), 1.0, 6.0, ((0, 4), (1, 8)))
    block_facet_keys = jax.random.split(jax.random.fold_in(key_of[1], 1), CGROUPS * FACETS * BLK_DEV // BLK_DEV)
    block_facet_turns = jax.random.permutation(jax.random.fold_in(key_of[1], 3), CGROUPS * FACETS * BLK_DEV // BLK_DEV)
    block_facet = jax.vmap(lambda own, number: deal_out(jax.random.fold_in(key_of[1], 2), own, number, BLK_DEV, FACETS, 1, CAP, 2))(block_facet_keys, block_facet_turns).reshape((CGROUPS, FACETS, BLK_DEV, 1))
    block_tile = with_ends(jax.random.randint(key_of[2], (CGROUPS, FACETS, BLK_DEV), 0, TT), jax.random.fold_in(key_of[2], 1), 0, TT - 1).astype(jnp.int32)
    vis_offset = with_ends(jax.random.randint(key_of[3], (CGROUPS, FACETS, BLK_DEV, VB), 0, OFFS * OFFS), jax.random.fold_in(key_of[3], 1), 0, (OFFS * OFFS) - 1).astype(jnp.int32)
    kernel_taps = jnp.clip(jax.random.uniform(key_of[4], (2, KT), jnp.float32, 0.19921875, 1.0), 0.19921875, 1.0).astype(jnp.bfloat16)
    return dict(voltages=voltages, block_facet=block_facet, block_tile=block_tile, vis_offset=vis_offset, kernel_taps=kernel_taps)


def kernel_rows(offsets, taps_row):
    cell_ids = jnp.arange(TILE, dtype=jnp.int32)
    distance = cell_ids[None, :, None] - offsets[:, None, :]
    weights_sum = jnp.zeros(distance.shape, jnp.float32)
    for tap_index in range(KT):
        weights_sum = weights_sum + jnp.where(distance == tap_index, taps_row[tap_index].astype(jnp.float32), jnp.float32(0.0))
    return weights_sum.astype(jnp.bfloat16)

def block_tiles(values, offsets, kernel_taps):
    along_u = kernel_rows(offsets // OFFS, kernel_taps[0])
    along_v = kernel_rows(offsets % OFFS, kernel_taps[1])
    weighted = (values[:, :, None, :].astype(jnp.float32) * along_v[:, None, :, :].astype(jnp.float32)).astype(jnp.bfloat16)
    weighted = weighted.reshape(values.shape[0], 2 * TILE, values.shape[2])
    return jnp.einsum('nux,nwx->nuw', along_u.astype(jnp.float32), weighted.astype(jnp.float32))

def reference(voltages, block_facet, block_tile, vis_offset, kernel_taps):
    per_channel = STATIONS * STATIONS // VB
    by_channel = jnp.transpose(voltages, (1, 0, 2))
    facet_rows = block_facet.reshape(CHANNELS, per_channel)
    tile_rows = block_tile.reshape(CHANNELS, per_channel)
    offset_rows = vis_offset.reshape(CHANNELS, per_channel, VB)
    station_ids = jnp.arange(STATIONS, dtype=jnp.int32)
    off_diagonal = (station_ids[:, None] != station_ids[None, :]).astype(jnp.float32)
    scale = 1.0 / math.sqrt(SAMPLES)

    def one_channel(grids, inputs):
        panel, facets_here, tiles_here, offsets_here = inputs
        whole = panel.astype(jnp.float32)
        swapped = jnp.concatenate([whole[:, SAMPLES:], -whole[:, :SAMPLES]], axis=1)
        real_vis = (jnp.dot(whole, whole.T, preferred_element_type=jnp.float32) * scale * off_diagonal).astype(jnp.bfloat16)
        imag_vis = (jnp.dot(swapped, whole.T, preferred_element_type=jnp.float32) * scale * off_diagonal).astype(jnp.bfloat16)
        values = jnp.stack([real_vis.reshape(per_channel, VB), imag_vis.reshape(per_channel, VB)], axis=1)
        tile_sums = block_tiles(values, offsets_here, kernel_taps).reshape(per_channel, 2 * TILE * TILE)
        targets = (facets_here * TT + tiles_here).astype(jnp.int32)
        return (grids + jax.ops.segment_sum(tile_sums, targets, num_segments=FACETS * TT), None)
    start_grids = jnp.zeros((FACETS * TT, 2 * TILE * TILE), jnp.float32)
    grids, leftover = lax.scan(one_channel, start_grids, (by_channel, facet_rows, tile_rows, offset_rows))
    shaped = grids.reshape(FACETS, TS, TS, TILE, 2, TILE)
    planes = jnp.transpose(shaped, (0, 4, 1, 3, 2, 5)).reshape(FACETS, 2, FG, FG)
    spectrum = jnp.fft.fft2(planes[:, 0] + 1j * planes[:, 1])
    norm_factor = 1.0 / math.sqrt(CHANNELS * STATIONS * STATIONS * KT * KT / FACETS)
    image = jnp.stack([jnp.real(spectrum), jnp.imag(spectrum)], axis=0) * norm_factor
    return image.reshape(2, FACETS * FG, FG).astype(jnp.float32)
```

```python
import functools
import math

import jax
import jax.numpy as jnp
import numpy as np
from jax import lax
from jax.experimental import pallas as pl
from jax.experimental.pallas import tpu as pltpu
from jax.sharding import PartitionSpec as P

VB = 128
TILE = 32
KT = 8
TS = 4
TT = 16
OFFS = 25
FG = TS * TILE

GROUP = 4
UNROLL = 16
CHUNKS = 4

F32, BF16, I32 = jnp.float32, jnp.bfloat16, jnp.int32
LAST_BY_LAST = (((1,), (1,)), ((), ()))


def group_lists(targets, target_count):
    count = targets.shape[0]
    block_ids = jnp.arange(count, dtype=I32)
    target_range = jnp.arange(target_count, dtype=I32)
    same = targets[:, None] == targets[None, :]
    position = jnp.sum((same & (block_ids[None, :] < block_ids[:, None])).astype(I32), axis=1)
    member = (targets[:, None] == target_range[None, :]).astype(I32)
    group_counts = (jnp.sum(member, axis=0) + GROUP - 1) // GROUP
    below = (target_range[:, None] < target_range[None, :]).astype(I32)
    first_group = jnp.sum(group_counts[:, None] * below, axis=0)
    slots = jnp.sum(member * first_group[None, :], axis=1) * GROUP + position
    most = (count + target_count * (GROUP - 1)) // GROUP
    most = -(-most // UNROLL) * UNROLL
    places = jnp.arange(most * GROUP, dtype=I32)
    listed = count + jnp.sum(
        jnp.where(slots[None, :] == places[:, None], block_ids[None, :] - count, 0), axis=1
    )
    groups = jnp.arange(most, dtype=I32)
    group_target = jnp.sum((groups[:, None] >= first_group[None, :]).astype(I32), axis=1) - 1
    turns = (jnp.sum(group_counts) + UNROLL - 1) // UNROLL
    return listed, group_target, turns


def grid_kernel(panels, first, last, listed, group_target, info, *refs):
    refs = list(refs)
    part_refs = [refs.pop(0) for _ in range(panels)]
    offset_ref = refs.pop(0)
    before_ref = None if first else refs.pop(0)
    tables = (refs.pop(0), refs.pop(0)) if last else None
    out_ref, whole, du_rows, dv_rows, re_rows, im_rows = refs[:6]
    cells = refs[6] if last else out_ref

    me = info[1]
    channels, rows, width = part_refs[0].shape
    stations = panels * rows
    samples = width // 2
    halves = stations // VB
    blocks = offset_ref.shape[0]

    if first:
        cells[...] = jnp.zeros_like(cells)
    else:
        cells[...] = before_ref[...]

    offsets = offset_ref[...]
    du = (offsets * 1311) >> 15
    du_rows[0:blocks] = du.astype(F32)
    dv_rows[0:blocks] = (offsets - du * OFFS).astype(F32)
    no_row = jnp.zeros((8, VB), F32)
    for row_ref in (du_rows, dv_rows, re_rows, im_rows):
        row_ref[blocks:] = no_row

    for step, part in enumerate(part_refs):
        start = pl.multiple_of(jnp.bitwise_xor(me, step) * rows, rows)
        for k in range(channels):
            whole[k, pl.ds(start, rows), :] = part[k]

    scale = 1.0 / math.sqrt(samples)
    diagonal = lax.broadcasted_iota(I32, (stations, stations), 0) == lax.broadcasted_iota(
        I32, (stations, stations), 1
    )
    for k in range(channels):
        x = whole[k]
        swapped = jnp.concatenate([x[:, samples:], -x[:, :samples]], axis=1)
        for row_ref, left in ((re_rows, x), (im_rows, swapped)):
            vis = lax.dot_general(left, x, LAST_BY_LAST, preferred_element_type=F32) * scale
            vis = jnp.where(diagonal, 0.0, vis).astype(BF16).astype(F32)
            for h in range(halves):
                row_ref[pl.ds(k * stations * halves + h, stations, stride=halves), :] = vis[
                    :, h * VB : (h + 1) * VB
                ]

    half = lax.broadcasted_iota(I32, (16, VB), 0).astype(F32)
    cell_ids = [(half + 16 * part).astype(BF16) for part in range(TILE // 16)]
    none = jnp.zeros((16, VB), BF16)
    ones = jnp.ones((16, VB), BF16)

    def spread(row_ref, n):
        return jnp.broadcast_to(row_ref[pl.ds(n, 1), :], (16, VB)).astype(BF16)

    def block_pair(n):
        du_n, dv_n = spread(du_rows, n), spread(dv_rows, n)
        re_n, im_n = spread(re_rows, n), spread(im_rows, n)
        along_u = [jnp.where(ids == du_n, ones, none) for ids in cell_ids]
        along_v = [jnp.where(ids == dv_n, re_n, none) for ids in cell_ids]
        along_v += [jnp.where(ids == dv_n, im_n, none) for ids in cell_ids]
        return jnp.concatenate(along_u, axis=0), jnp.concatenate(along_v, axis=0)

    def turn(index, carry):
        sums = []
        for q in range(UNROLL):
            g = index * UNROLL + q
            pairs = [block_pair(listed[g * GROUP + p]) for p in range(GROUP)]
            left = jnp.concatenate([a for a, b in pairs], axis=1)
            right = jnp.concatenate([b for a, b in pairs], axis=1)
            sums.append(
                (g, lax.dot_general(left, right, LAST_BY_LAST, preferred_element_type=F32))
            )
        for g, total in sums:
            cells[group_target[g]] += total
        return carry

    lax.fori_loop(0, info[0], turn, 0)

    if last:
        row_table, column_table = tables
        facets = cells.shape[0] // TT

        def transform(f, carry):
            grid = jnp.concatenate(
                [
                    jnp.concatenate([cells[f * TT + tu * TS + tv] for tv in range(TS)], axis=1)
                    for tu in range(TS)
                ],
                axis=0,
            )
            part = jnp.dot(
                row_table[...], grid, precision=lax.Precision.HIGHEST, preferred_element_type=F32
            )
            both = jnp.concatenate([part[:FG], part[FG:]], axis=1)
            image = jnp.dot(
                both, column_table[...], precision=lax.Precision.HIGHEST, preferred_element_type=F32
            )
            out_ref[pl.ds(pl.multiple_of(f * FG, FG), FG), :] = image.astype(out_ref.dtype)
            return carry

        lax.fori_loop(0, facets, transform, 0)


def grid_call(info, lists, parts, offsets, before, tables, target_count):
    listed, group_target = lists
    panels = len(parts)
    channels, rows, width = parts[0].shape
    blocks = offsets.shape[0]
    first, last = before is None, tables is not None
    operands = list(parts) + [offsets]
    if not first:
        operands.append(before)
    if last:
        operands += list(tables)
    cells = (target_count, TILE, 2 * TILE)
    scratch = [pltpu.VMEM((channels, panels * rows, width), BF16)]
    scratch += [pltpu.VMEM((blocks + 8, VB), F32)] * 4
    if last:
        scratch.append(pltpu.VMEM(cells, F32))
        out = jax.ShapeDtypeStruct((target_count // TT * FG, 2 * FG), BF16)
    else:
        out = jax.ShapeDtypeStruct(cells, F32)
    whole = lambda shape: pl.BlockSpec(shape, lambda i, *_: (0,) * len(shape))
    return pl.pallas_call(
        functools.partial(grid_kernel, panels, first, last),
        grid_spec=pltpu.PrefetchScalarGridSpec(
            num_scalar_prefetch=3,
            grid=(1,),
            in_specs=[whole(x.shape) for x in operands],
            out_specs=whole(out.shape),
            scratch_shapes=scratch,
        ),
        out_shape=out,
        compiler_params=pltpu.CompilerParams(vmem_limit_bytes=48 << 20),
    )(listed, group_target, info, *operands)


def transform_tables():
    ids = np.arange(FG)
    angles = (ids[:, None] * ids[None, :] % FG) * (2.0 * math.pi / FG)
    cosine, sine = np.cos(angles), -np.sin(angles)
    row_table = np.concatenate([cosine, sine], axis=0)
    straight = np.concatenate([cosine, sine], axis=1).reshape(TS, 1, TILE, 2 * FG)
    turned = np.concatenate([-sine, cosine], axis=1).reshape(TS, 1, TILE, 2 * FG)
    real = np.concatenate([straight, turned], axis=1).reshape(2 * FG, 2 * FG)
    imag = np.concatenate([turned, -straight], axis=1).reshape(2 * FG, 2 * FG)
    column_table = np.concatenate([real, imag], axis=0)
    return row_table.astype(np.float32), column_table.astype(np.float32)


def taps_transform(taps_row):
    index_ids = jnp.arange(FG, dtype=I32)
    phases = index_ids[:, None] * jnp.arange(KT, dtype=I32)[None, :] % FG
    angles = phases.astype(F32) * (2.0 * math.pi / FG)
    taps = taps_row.astype(F32)[None, :]
    return jnp.sum(jnp.cos(angles) * taps, axis=1), -jnp.sum(jnp.sin(angles) * taps, axis=1)


def body(voltages, block_facet, block_tile, vis_offset, kernel_taps):
    facets = lax.axis_size("stn")
    chan_count = lax.axis_size("chan")
    me = lax.axis_index("stn")
    rows, all_channels, width = voltages.shape
    channels = all_channels // facets
    stations = rows * facets
    blocks = vis_offset.shape[2]
    target_count = facets * TT

    by_channel = jnp.transpose(voltages, (1, 0, 2)).reshape(facets, channels, rows, width)
    step = channels // CHUNKS
    parts = []
    for c in range(CHUNKS):
        got = []
        for s in range(facets):
            piece = lax.dynamic_slice(
                by_channel, (jnp.bitwise_xor(me, s), c * step, 0, 0), (1, step, rows, width)
            ).reshape(step, rows, width)
            if s:
                piece = lax.ppermute(piece, "stn", [(i, i ^ s) for i in range(facets)])
            got.append(piece)
        parts.append(got)

    offsets = vis_offset.reshape(CHUNKS, blocks // CHUNKS, VB)
    targets = (block_facet.reshape(CHUNKS, -1) * TT + block_tile.reshape(CHUNKS, -1)).astype(I32)
    tables = tuple(jnp.asarray(t) for t in transform_tables())
    cells = None
    for c in range(CHUNKS):
        listed, group_target, turns = group_lists(targets[c], target_count)
        info = jnp.stack([turns, me]).astype(I32)
        cells = grid_call(
            info,
            (listed, group_target),
            parts[c],
            offsets[c],
            cells,
            tables if c == CHUNKS - 1 else None,
            target_count,
        )

    row_count = FG // chan_count
    pieces = cells.reshape(facets * chan_count, row_count, 2 * FG)
    pieces = lax.all_to_all(pieces, ("stn", "chan"), split_axis=0, concat_axis=0, tiled=True)
    image = jnp.sum(pieces.astype(F32), axis=0)
    real, imag = image[:, :FG], image[:, FG:]

    channels_all = all_channels * chan_count
    norm_factor = 1.0 / math.sqrt(channels_all * stations * stations * KT * KT / facets)
    u_real, u_imag = taps_transform(kernel_taps[0])
    v_real, v_imag = taps_transform(kernel_taps[1])
    first_row = lax.axis_index("chan") * row_count
    u_real = lax.dynamic_slice_in_dim(u_real, first_row, row_count)[:, None] * norm_factor
    u_imag = lax.dynamic_slice_in_dim(u_imag, first_row, row_count)[:, None] * norm_factor
    w_real = u_real * v_real[None, :] - u_imag * v_imag[None, :]
    w_imag = u_real * v_imag[None, :] + u_imag * v_real[None, :]
    return jnp.stack([real * w_real - imag * w_imag, real * w_imag + imag * w_real], axis=0)


def solution(mesh):
    placed = (
        P("stn", "chan", None),
        P("chan", "stn", None, None),
        P("chan", "stn", None),
        P("chan", "stn", None, None),
        P(),
    )
    return jax.shard_map(
        body, mesh=mesh, in_specs=placed, out_specs=P(None, ("stn", "chan"), None), check_vma=False
    )
```

```python
import functools
import math

import jax
import jax.numpy as jnp
import ml_dtypes
import numpy as np
from jax import lax
from jax.experimental import pallas as pl
from jax.experimental.pallas import tpu as pltpu
from jax.sharding import PartitionSpec as P

VB = 128
TILE = 32
KT = 8
TS = 4
TT = 16
OFFS = 25
FG = TS * TILE

GROUP = 4
UNROLL = 32
CHUNK_ENDS = (2, 4)

F32, BF16, I32 = jnp.float32, jnp.bfloat16, jnp.int32
LAST_BY_LAST = (((1,), (1,)), ((), ()))


def whole_block(shape):
    return pl.BlockSpec(shape, lambda i, *_: (0,) * len(shape))


def group_lists(targets, target_count):
    count = targets.shape[0]
    block_ids = jnp.arange(count, dtype=I32)
    target_range = jnp.arange(target_count, dtype=I32)
    same = targets[:, None] == targets[None, :]
    position = jnp.sum((same & (block_ids[None, :] < block_ids[:, None])).astype(I32), axis=1)
    member = (targets[:, None] == target_range[None, :]).astype(I32)
    group_counts = (jnp.sum(member, axis=0) + GROUP - 1) // GROUP
    below = (target_range[:, None] < target_range[None, :]).astype(I32)
    first_group = jnp.sum(group_counts[:, None] * below, axis=0)
    slots = jnp.sum(member * first_group[None, :], axis=1) * GROUP + position
    most = (count + target_count * (GROUP - 1)) // GROUP
    most = -(-most // UNROLL) * UNROLL
    places = jnp.arange(most * GROUP, dtype=I32)
    listed = count + jnp.sum(
        jnp.where(slots[None, :] == places[:, None], block_ids[None, :] - count, 0), axis=1
    )
    groups = jnp.arange(most, dtype=I32)
    group_target = jnp.sum((groups[:, None] >= first_group[None, :]).astype(I32), axis=1) - 1
    turns = (jnp.sum(group_counts) + UNROLL - 1) // UNROLL
    return listed, group_target, turns


def two_halves(x):
    high = x.astype(BF16)
    return high, (x - high.astype(F32)).astype(BF16)


def halves_of(table_ref):
    return table_ref[0], table_ref[1]


def split_dot(left, right):
    dot = functools.partial(jnp.dot, preferred_element_type=F32)
    return dot(left[0], right[0]) + (dot(left[0], right[1]) + dot(left[1], right[0]))


def grid_kernel(panels, first, last, listed, group_target, info, *refs):
    refs = list(refs)
    part_refs = [refs.pop(0) for _ in range(panels)]
    offset_ref = refs.pop(0)
    before_ref = None if first else refs.pop(0)
    tables = (refs.pop(0), refs.pop(0)) if last else None
    out_ref, whole, du_rows, dv_rows, re_rows, im_rows = refs[:6]
    cells = refs[6] if last else out_ref

    me = info[1]
    channels, rows, width = part_refs[0].shape
    stations = panels * rows
    samples = width // 2
    halves = stations // VB
    blocks = offset_ref.shape[0]

    if first:
        cells[...] = jnp.zeros_like(cells)
    else:
        cells[...] = before_ref[...]

    offsets = offset_ref[...]
    du = (offsets * 1311) >> 15
    du_rows[0:blocks] = du.astype(F32)
    dv_rows[0:blocks] = (offsets - du * OFFS).astype(F32)
    no_row = jnp.zeros((8, VB), F32)
    for row_ref in (du_rows, dv_rows, re_rows, im_rows):
        row_ref[blocks:] = no_row

    for step, part in enumerate(part_refs):
        start = pl.multiple_of(jnp.bitwise_xor(me, step) * rows, rows)
        for k in range(channels):
            whole[k, pl.ds(start, rows), :] = part[k]

    scale = 1.0 / math.sqrt(samples)
    diagonal = lax.broadcasted_iota(I32, (stations, stations), 0) == lax.broadcasted_iota(
        I32, (stations, stations), 1
    )
    for k in range(channels):
        x = whole[k]
        swapped = jnp.concatenate([x[:, samples:], -x[:, :samples]], axis=1)
        for row_ref, left in ((re_rows, x), (im_rows, swapped)):
            vis = lax.dot_general(left, x, LAST_BY_LAST, preferred_element_type=F32) * scale
            vis = jnp.where(diagonal, 0.0, vis).astype(BF16).astype(F32)
            for h in range(halves):
                row_ref[pl.ds(k * stations * halves + h, stations, stride=halves), :] = vis[
                    :, h * VB : (h + 1) * VB
                ]

    half = lax.broadcasted_iota(I32, (16, VB), 0).astype(F32)
    cell_ids = [(half + 16 * part).astype(BF16) for part in range(TILE // 16)]
    none = jnp.zeros((16, VB), BF16)
    ones = jnp.ones((16, VB), BF16)

    def spread(row_ref, n):
        return jnp.broadcast_to(row_ref[pl.ds(n, 1), :], (16, VB)).astype(BF16)

    def block_pair(n):
        du_n, dv_n = spread(du_rows, n), spread(dv_rows, n)
        re_n, im_n = spread(re_rows, n), spread(im_rows, n)
        along_u = [jnp.where(ids == du_n, ones, none) for ids in cell_ids]
        along_v = [jnp.where(ids == dv_n, re_n, none) for ids in cell_ids]
        along_v += [jnp.where(ids == dv_n, im_n, none) for ids in cell_ids]
        return jnp.concatenate(along_u, axis=0), jnp.concatenate(along_v, axis=0)

    def turn(index, carry):
        sums = []
        for q in range(UNROLL):
            g = index * UNROLL + q
            pairs = [block_pair(listed[g * GROUP + p]) for p in range(GROUP)]
            left = jnp.concatenate([a for a, b in pairs], axis=1)
            right = jnp.concatenate([b for a, b in pairs], axis=1)
            sums.append(
                (g, lax.dot_general(left, right, LAST_BY_LAST, preferred_element_type=F32))
            )
        for g, total in sums:
            cells[group_target[g]] += total
        return carry

    lax.fori_loop(0, info[0], turn, 0)

    if last:
        row_table, column_table = tables
        facets = cells.shape[0] // TT
        grid = jnp.concatenate(
            [
                jnp.concatenate(
                    [
                        cells[f * TT + tu * TS + tv]
                        for f in range(facets)
                        for tv in range(TS)
                    ],
                    axis=1,
                )
                for tu in range(TS)
            ],
            axis=0,
        )
        columns = split_dot(halves_of(row_table), two_halves(grid))
        both = jnp.concatenate(
            [
                jnp.concatenate(
                    [
                        columns[q * FG : (q + 1) * FG, f * 2 * FG : (f + 1) * 2 * FG]
                        for q in range(2)
                    ],
                    axis=1,
                )
                for f in range(facets)
            ],
            axis=0,
        )
        image = split_dot(two_halves(both), halves_of(column_table))
        out_ref[...] = image.astype(out_ref.dtype)


def deal_kernel(chunks, info, voltage_ref, *refs):
    outs, wide = refs[:-1], refs[-1]
    rows, all_channels, width = voltage_ref.shape
    facets = len(outs) // len(chunks)
    channels = all_channels // facets
    lanes = wide.shape[0]
    for q in range(rows):
        row = voltage_ref[q].astype(F32)
        for t in range(lanes):
            wide[t, q * all_channels : (q + 1) * all_channels, :] = row[:, t * VB : (t + 1) * VB]
    for c, (begin, end) in enumerate(chunks):
        for s in range(facets):
            first = jnp.bitwise_xor(info[0], s) * channels
            for k in range(begin, end):
                taken = [
                    wide[t, pl.ds(first + k, rows, stride=all_channels), :] for t in range(lanes)
                ]
                outs[c * facets + s][k - begin] = jnp.concatenate(taken, axis=1).astype(BF16)


def deal_channels(voltages, me, facets, chunks):
    rows, all_channels, width = voltages.shape
    shapes = [(end - begin, rows, width) for begin, end in chunks for s in range(facets)]
    return pl.pallas_call(
        functools.partial(deal_kernel, chunks),
        grid_spec=pltpu.PrefetchScalarGridSpec(
            num_scalar_prefetch=1,
            grid=(1,),
            in_specs=[whole_block(voltages.shape)],
            out_specs=[whole_block(shape) for shape in shapes],
            scratch_shapes=[pltpu.VMEM((width // VB, rows * all_channels, VB), F32)],
        ),
        out_shape=[jax.ShapeDtypeStruct(shape, voltages.dtype) for shape in shapes],
        compiler_params=pltpu.CompilerParams(vmem_limit_bytes=32 << 20),
    )(me.reshape(1).astype(I32), voltages)


def grid_call(info, lists, parts, offsets, before, tables, target_count):
    listed, group_target = lists
    panels = len(parts)
    channels, rows, width = parts[0].shape
    blocks = offsets.shape[0]
    first, last = before is None, tables is not None
    operands = list(parts) + [offsets]
    if not first:
        operands.append(before)
    if last:
        operands += list(tables)
    cells = (target_count, TILE, 2 * TILE)
    scratch = [pltpu.VMEM((channels, panels * rows, width), BF16)]
    scratch += [pltpu.VMEM((blocks + 8, VB), F32)] * 4
    if last:
        scratch.append(pltpu.VMEM(cells, F32))
        out = jax.ShapeDtypeStruct((target_count // TT * FG, 2 * FG), BF16)
    else:
        out = jax.ShapeDtypeStruct(cells, F32)
    return pl.pallas_call(
        functools.partial(grid_kernel, panels, first, last),
        grid_spec=pltpu.PrefetchScalarGridSpec(
            num_scalar_prefetch=3,
            grid=(1,),
            in_specs=[whole_block(x.shape) for x in operands],
            out_specs=whole_block(out.shape),
            scratch_shapes=scratch,
        ),
        out_shape=out,
        compiler_params=pltpu.CompilerParams(vmem_limit_bytes=48 << 20),
    )(listed, group_target, info, *operands)


def split_table(table):
    high = table.astype(ml_dtypes.bfloat16)
    return high, (table - high.astype(np.float64)).astype(ml_dtypes.bfloat16)


def transform_tables():
    ids = np.arange(FG)
    angles = (ids[:, None] * ids[None, :] % FG) * (2.0 * math.pi / FG)
    cosine, sine = np.cos(angles), -np.sin(angles)
    row_table = np.concatenate([cosine, sine], axis=0)
    straight = np.concatenate([cosine, sine], axis=1).reshape(TS, 1, TILE, 2 * FG)
    turned = np.concatenate([-sine, cosine], axis=1).reshape(TS, 1, TILE, 2 * FG)
    real = np.concatenate([straight, turned], axis=1).reshape(2 * FG, 2 * FG)
    imag = np.concatenate([turned, -straight], axis=1).reshape(2 * FG, 2 * FG)
    column_table = np.concatenate([real, imag], axis=0)
    return tuple(np.stack(split_table(t)) for t in (row_table, column_table))


def taps_transform(taps_row):
    index_ids = jnp.arange(FG, dtype=I32)
    phases = index_ids[:, None] * jnp.arange(KT, dtype=I32)[None, :] % FG
    angles = phases.astype(F32) * (2.0 * math.pi / FG)
    taps = taps_row.astype(F32)[None, :]
    return jnp.sum(jnp.cos(angles) * taps, axis=1), -jnp.sum(jnp.sin(angles) * taps, axis=1)


def body(voltages, block_facet, block_tile, vis_offset, kernel_taps):
    facets = lax.axis_size("stn")
    chan_count = lax.axis_size("chan")
    me = lax.axis_index("stn")
    rows, all_channels, width = voltages.shape
    channels = all_channels // facets
    stations = rows * facets
    blocks = vis_offset.shape[2]
    target_count = facets * TT

    ends = [channels * e // 4 for e in CHUNK_ENDS]
    chunks = list(zip([0] + ends[:-1], ends))
    pieces = deal_channels(voltages, me, facets, chunks)
    parts = []
    for c in range(len(chunks)):
        got = [pieces[c * facets]]
        for s in range(facets - 1, 0, -1):
            pairs = [(i, i ^ s) for i in range(facets)]
            got.insert(1, lax.ppermute(pieces[c * facets + s], "stn", pairs))
        parts.append(got)

    per_channel = blocks // channels
    offsets = vis_offset.reshape(blocks, VB)
    targets = (block_facet.reshape(blocks) * TT + block_tile.reshape(blocks)).astype(I32)
    tables = tuple(jnp.asarray(t) for t in transform_tables())
    cells = None
    for (begin, end), got in zip(chunks, parts):
        held = slice(begin * per_channel, end * per_channel)
        chunk_targets = targets[held]
        listed, group_target, turns = group_lists(chunk_targets, target_count)
        info = jnp.stack([turns, me]).astype(I32)
        cells = grid_call(
            info,
            (listed, group_target),
            got,
            offsets[held],
            cells,
            tables if end == channels else None,
            target_count,
        )

    row_count = FG // chan_count
    pieces = cells.reshape(facets * chan_count, row_count, 2 * FG)
    pieces = lax.all_to_all(pieces, ("stn", "chan"), split_axis=0, concat_axis=0, tiled=True)
    channels_all = all_channels * chan_count
    norm_factor = 1.0 / math.sqrt(channels_all * stations * stations * KT * KT / facets)
    u_real, u_imag = taps_transform(kernel_taps[0])
    v_real, v_imag = taps_transform(kernel_taps[1])
    first_row = lax.axis_index("chan") * row_count
    u_real = lax.dynamic_slice_in_dim(u_real, first_row, row_count)[:, None] * norm_factor
    u_imag = lax.dynamic_slice_in_dim(u_imag, first_row, row_count)[:, None] * norm_factor
    w_real = u_real * v_real[None, :] - u_imag * v_imag[None, :]
    w_imag = u_real * v_imag[None, :] + u_imag * v_real[None, :]
    of_real = jnp.stack([w_real, w_imag])
    of_imag = jnp.stack([-w_imag, w_real])

    image = jnp.sum(pieces.astype(F32), axis=0)
    return image[None, :, :FG] * of_real + image[None, :, FG:] * of_imag


def solution(mesh):
    placed = (
        P("stn", "chan", None),
        P("chan", "stn", None, None),
        P("chan", "stn", None),
        P("chan", "stn", None, None),
        P(),
    )
    return jax.shard_map(
        body, mesh=mesh, in_specs=placed, out_specs=P(None, ("stn", "chan"), None), check_vma=False
    )
```

```python
import functools
import math

import jax
import jax.numpy as jnp
import ml_dtypes
import numpy as np
from jax import lax
from jax.experimental import pallas as pl
from jax.experimental.pallas import tpu as pltpu
from jax.sharding import PartitionSpec as P

VB = 128
TILE = 32
KT = 8
TS = 4
TT = 16
OFFS = 25
FG = TS * TILE

GROUP = 4
UNROLL = 48
CHUNK_ENDS = (2, 4)

F32, BF16, I32 = jnp.float32, jnp.bfloat16, jnp.int32
LAST_BY_LAST = (((1,), (1,)), ((), ()))


def whole_block(shape):
    return pl.BlockSpec(shape, lambda i, *_: (0,) * len(shape))


def list_places(count, target_count):
    most = (count + target_count * (GROUP - 1)) // GROUP
    most = -(-most // UNROLL) * UNROLL
    block_rows = -(-most * GROUP // VB)
    group_rows = -(-most // VB)
    return block_rows, group_rows, -(-(block_rows + group_rows + 1) // 8) * 8


def late_steps(panels):
    return range((panels + 1) // 2, panels - 1)


def early_blocks(shape, ids, me):
    panels, rows, halves = shape
    in_channel = ids - jnp.floor(ids * (1.0 / (panels * rows * halves))) * (panels * rows * halves)
    station = jnp.floor(in_channel * (1.0 / halves))
    panel = jnp.floor(station * (1.0 / rows)).astype(I32)
    step = jnp.bitwise_xor(panel, me)
    late = late_steps(panels)
    held = jnp.logical_or(step < late.start, step >= late.stop)
    own = in_channel - station * halves == (me * rows // VB).astype(F32)
    return jnp.logical_and(own, held).astype(F32)


def list_chunk(first_row, rows, listed_count, choice, shape, target_count, refs):
    facet_ref, tile_ref, out_ref = refs
    count = rows * VB
    block_rows, group_rows, _ = list_places(listed_count, target_count)
    exact = functools.partial(
        jnp.dot, precision=lax.Precision.HIGHEST, preferred_element_type=F32
    )
    dot = functools.partial(jnp.dot, preferred_element_type=F32)
    iota = lambda shape, dim: lax.broadcasted_iota(I32, shape, dim).astype(F32)
    target_ids = iota((target_count, VB), 0)
    square = (VB, VB)
    before = (iota(square, 0) < iota(square, 1)).astype(BF16)
    ones = jnp.ones(square, BF16)
    ids = iota((1, VB), 1)

    members, positions = [], []
    counted = jnp.zeros((target_count, VB), F32)
    for q in range(rows):
        r = first_row + q
        targets = (facet_ref[r : r + 1, :] * TT + tile_ref[r : r + 1, :]).astype(F32)
        chosen = jnp.ones((1, VB), F32)
        if choice is not None:
            early = early_blocks(shape, ids + q * VB, lax.axis_index("stn"))
            chosen = early if choice else 1.0 - early
        member = (target_ids == targets).astype(F32) * chosen
        members.append((member, chosen))
        positions.append(counted + dot(member.astype(BF16), before))
        counted = counted + dot(member.astype(BF16), ones)
    groups = jnp.floor((counted + (GROUP - 1)) * (1.0 / GROUP))
    lower = iota((target_count, target_count), 0) > iota((target_count, target_count), 1)
    first_group = exact(lower.astype(F32), groups)

    row_ids = iota((block_rows, VB), 0)
    lane_ids = iota(square, 0)
    held = jnp.zeros((3 * block_rows, VB), F32)
    for q, ((member, chosen), position) in enumerate(zip(members, positions)):
        slots = jnp.sum(member * (first_group * GROUP + position), axis=0, keepdims=True)
        slot_rows = jnp.floor(slots * (1.0 / VB))
        in_row = (row_ids == slot_rows).astype(F32) * chosen
        in_lane = (lane_ids == slots - slot_rows * VB).astype(BF16)
        left = jnp.concatenate([in_row, in_row * ids, in_row * q], axis=0).astype(BF16)
        held = held + lax.dot_general(left, in_lane, LAST_BY_LAST, preferred_element_type=F32)
    taken, low, high = (held[k * block_rows : (k + 1) * block_rows] for k in range(3))
    listed = jnp.where(taken > 0.5, low + VB * high, count)

    out_ref[...] = jnp.zeros_like(out_ref)
    out_ref[0:block_rows, :] = listed.astype(I32)
    for r in range(group_rows):
        group_ids = iota((target_count, VB), 1) + r * VB
        named = jnp.sum((group_ids >= first_group).astype(F32), axis=0, keepdims=True) - 1.0
        out_ref[block_rows + r : block_rows + r + 1, :] = named.astype(I32)
    total = jnp.sum(groups, axis=0, keepdims=True)
    turns = jnp.floor((total + (UNROLL - 1)) * (1.0 / UNROLL))
    last = block_rows + group_rows
    out_ref[last : last + 1, :] = turns.astype(I32)


def group_lists(facet_ids, tile_ids, wanted, shape, target_count):
    def kernel(facet_ref, tile_ref, *out_refs):
        for (first_row, rows, count, choice), out_ref in zip(wanted, out_refs):
            refs = (facet_ref, tile_ref, out_ref)
            list_chunk(first_row, rows, count, choice, shape, target_count, refs)

    shapes = [(list_places(count, target_count)[2], VB) for _, _, count, _ in wanted]
    lists = pl.pallas_call(
        kernel,
        grid=(1,),
        in_specs=[whole_block(facet_ids.shape), whole_block(tile_ids.shape)],
        out_specs=[whole_block(shape) for shape in shapes],
        out_shape=[jax.ShapeDtypeStruct(shape, I32) for shape in shapes],
        compiler_params=pltpu.CompilerParams(vmem_limit_bytes=32 << 20),
    )(facet_ids, tile_ids)
    return [x.reshape(-1) for x in lists]


def two_halves(x):
    high = x.astype(BF16)
    return high, (x - high.astype(F32)).astype(BF16)


def halves_of(table_ref):
    return table_ref[0], table_ref[1]


def split_dot(left, right):
    dot = functools.partial(jnp.dot, preferred_element_type=F32)
    return dot(left[0], right[0]) + (dot(left[0], right[1]) + dot(left[1], right[0]))


def grid_kernel(steps, first, last, places, listed, *refs):
    refs = list(refs)
    part_refs = [refs.pop(0) for _ in steps]
    offset_ref = refs.pop(0)
    before_ref = None if first else refs.pop(0)
    tables = (refs.pop(0), refs.pop(0)) if last else None
    out_ref, whole, du_rows, dv_rows, re_rows, im_rows = refs[:6]
    cells = refs[6] if last else out_ref

    me = lax.axis_index("stn")
    targets_at, turns_at = places[0] * VB, (places[0] + places[1]) * VB
    channels, rows, width = part_refs[0].shape
    stations = whole.shape[1]
    samples = width // 2
    halves = stations // VB
    blocks = offset_ref.shape[0]

    if first:
        cells[...] = jnp.zeros_like(cells)
    else:
        cells[...] = before_ref[...]

    offsets = offset_ref[...]
    du = (offsets * 1311) >> 15
    du_rows[0:blocks] = du.astype(F32)
    dv_rows[0:blocks] = (offsets - du * OFFS).astype(F32)
    no_row = jnp.zeros((8, VB), F32)
    for row_ref in (du_rows, dv_rows, re_rows, im_rows):
        row_ref[blocks:] = no_row

    if len(steps) * rows < stations:
        whole[...] = jnp.zeros_like(whole)
    for step, part in zip(steps, part_refs):
        start = pl.multiple_of(jnp.bitwise_xor(me, step) * rows, rows)
        for k in range(channels):
            whole[k, pl.ds(start, rows), :] = part[k]

    scale = 1.0 / math.sqrt(samples)
    diagonal = lax.broadcasted_iota(I32, (stations, stations), 0) == lax.broadcasted_iota(
        I32, (stations, stations), 1
    )
    for k in range(channels):
        x = whole[k]
        swapped = jnp.concatenate([x[:, samples:], -x[:, :samples]], axis=1)
        for row_ref, left in ((re_rows, x), (im_rows, swapped)):
            vis = lax.dot_general(left, x, LAST_BY_LAST, preferred_element_type=F32) * scale
            vis = jnp.where(diagonal, 0.0, vis).astype(BF16).astype(F32)
            for h in range(halves):
                row_ref[pl.ds(k * stations * halves + h, stations, stride=halves), :] = vis[
                    :, h * VB : (h + 1) * VB
                ]

    half = lax.broadcasted_iota(I32, (16, VB), 0).astype(F32)
    cell_ids = [(half + 16 * part).astype(BF16) for part in range(TILE // 16)]
    none = jnp.zeros((16, VB), BF16)
    ones = jnp.ones((16, VB), BF16)

    def spread(row_ref, n):
        return jnp.broadcast_to(row_ref[pl.ds(n, 1), :], (16, VB)).astype(BF16)

    def block_pair(n):
        du_n, dv_n = spread(du_rows, n), spread(dv_rows, n)
        re_n, im_n = spread(re_rows, n), spread(im_rows, n)
        along_u = [jnp.where(ids == du_n, ones, none) for ids in cell_ids]
        along_v = [jnp.where(ids == dv_n, re_n, none) for ids in cell_ids]
        along_v += [jnp.where(ids == dv_n, im_n, none) for ids in cell_ids]
        return jnp.concatenate(along_u, axis=0), jnp.concatenate(along_v, axis=0)

    def turn(index, carry):
        sums = []
        for q in range(UNROLL):
            g = index * UNROLL + q
            pairs = [block_pair(listed[g * GROUP + p]) for p in range(GROUP)]
            left = jnp.concatenate([a for a, b in pairs], axis=1)
            right = jnp.concatenate([b for a, b in pairs], axis=1)
            sums.append(
                (g, lax.dot_general(left, right, LAST_BY_LAST, preferred_element_type=F32))
            )
        for g, total in sums:
            cells[listed[targets_at + g]] += total
        return carry

    lax.fori_loop(0, listed[turns_at], turn, 0)

    if last:
        row_table, column_table = tables
        facets = cells.shape[0] // TT
        grid = jnp.concatenate(
            [
                jnp.concatenate(
                    [
                        cells[f * TT + tu * TS + tv]
                        for f in range(facets)
                        for tv in range(TS)
                    ],
                    axis=1,
                )
                for tu in range(TS)
            ],
            axis=0,
        )
        columns = split_dot(halves_of(row_table), two_halves(grid))
        both = jnp.concatenate(
            [
                jnp.concatenate(
                    [
                        columns[q * FG : (q + 1) * FG, f * 2 * FG : (f + 1) * 2 * FG]
                        for q in range(2)
                    ],
                    axis=1,
                )
                for f in range(facets)
            ],
            axis=0,
        )
        image = split_dot(two_halves(both), halves_of(column_table))
        out_ref[...] = image.astype(out_ref.dtype)


def farthest_first(panels):
    return [panels - 1] + list(range(1, panels - 1))


def deal_kernel(begin, end, facets, voltage_ref, *refs):
    outs, wide = refs[-facets - 1 : -1], refs[-1]
    rows, all_channels, width = voltage_ref.shape
    channels = all_channels // facets
    lanes = wide.shape[0]
    for q in range(rows):
        row = voltage_ref[q].astype(F32)
        for t in range(lanes):
            wide[t, q * all_channels : (q + 1) * all_channels, :] = row[:, t * VB : (t + 1) * VB]
    for s in range(facets):
        first = jnp.bitwise_xor(lax.axis_index("stn"), s) * channels
        for k in range(begin, end):
            taken = [wide[t, pl.ds(first + k, rows, stride=all_channels), :] for t in range(lanes)]
            outs[s][k - begin] = jnp.concatenate(taken, axis=1).astype(BF16)


def deal_channels(voltages, facets, begin, end, after):
    rows, all_channels, width = voltages.shape
    shape = (end - begin, rows, width)
    return pl.pallas_call(
        functools.partial(deal_kernel, begin, end, facets),
        grid=(1,),
        in_specs=[whole_block(voltages.shape)] + [pl.BlockSpec(memory_space=pl.ANY)] * len(after),
        out_specs=[whole_block(shape)] * facets,
        scratch_shapes=[pltpu.VMEM((width // VB, rows * all_channels, VB), F32)],
        out_shape=[jax.ShapeDtypeStruct(shape, voltages.dtype)] * facets,
        compiler_params=pltpu.CompilerParams(vmem_limit_bytes=32 << 20),
    )(voltages, *after)


def grid_call(listed, listed_count, stations, steps, parts, offsets, before, tables, target_count):
    channels, rows, width = parts[0].shape
    blocks = offsets.shape[0]
    first, last = before is None, tables is not None
    operands = list(parts) + [offsets]
    if not first:
        operands.append(before)
    if last:
        operands += list(tables)
    cells = (target_count, TILE, 2 * TILE)
    scratch = [pltpu.VMEM((channels, stations, width), BF16)]
    scratch += [pltpu.VMEM((blocks + 8, VB), F32)] * 4
    if last:
        scratch.append(pltpu.VMEM(cells, F32))
        out = jax.ShapeDtypeStruct((target_count // TT * FG, 2 * FG), BF16)
    else:
        out = jax.ShapeDtypeStruct(cells, F32)
    return pl.pallas_call(
        functools.partial(
            grid_kernel, steps, first, last, list_places(listed_count, target_count)
        ),
        grid_spec=pltpu.PrefetchScalarGridSpec(
            num_scalar_prefetch=1,
            grid=(1,),
            in_specs=[whole_block(x.shape) for x in operands],
            out_specs=whole_block(out.shape),
            scratch_shapes=scratch,
        ),
        out_shape=out,
        compiler_params=pltpu.CompilerParams(vmem_limit_bytes=48 << 20),
    )(listed, *operands)


def split_table(table):
    high = table.astype(ml_dtypes.bfloat16)
    return high, (table - high.astype(np.float64)).astype(ml_dtypes.bfloat16)


def transform_tables():
    ids = np.arange(FG)
    angles = (ids[:, None] * ids[None, :] % FG) * (2.0 * math.pi / FG)
    cosine, sine = np.cos(angles), -np.sin(angles)
    row_table = np.concatenate([cosine, sine], axis=0)
    straight = np.concatenate([cosine, sine], axis=1).reshape(TS, 1, TILE, 2 * FG)
    turned = np.concatenate([-sine, cosine], axis=1).reshape(TS, 1, TILE, 2 * FG)
    real = np.concatenate([straight, turned], axis=1).reshape(2 * FG, 2 * FG)
    imag = np.concatenate([turned, -straight], axis=1).reshape(2 * FG, 2 * FG)
    column_table = np.concatenate([real, imag], axis=0)
    return tuple(np.stack(split_table(t)) for t in (row_table, column_table))


def taps_transform(taps_row):
    index_ids = jnp.arange(FG, dtype=I32)
    phases = index_ids[:, None] * jnp.arange(KT, dtype=I32)[None, :] % FG
    angles = phases.astype(F32) * (2.0 * math.pi / FG)
    taps = taps_row.astype(F32)[None, :]
    return jnp.sum(jnp.cos(angles) * taps, axis=1), -jnp.sum(jnp.sin(angles) * taps, axis=1)


def body(voltages, block_facet, block_tile, vis_offset, kernel_taps):
    facets = lax.axis_size("stn")
    chan_count = lax.axis_size("chan")
    rows, all_channels, width = voltages.shape
    channels = all_channels // facets
    stations = rows * facets
    blocks = vis_offset.shape[2]
    target_count = facets * TT

    ends = [channels * e // 4 for e in CHUNK_ENDS]
    chunks = list(zip([0] + ends[:-1], ends))
    per_channel = blocks // channels
    offsets = vis_offset.reshape(blocks, VB)
    halves = stations // VB
    early = [0] + [t for t in farthest_first(facets) if t not in late_steps(facets)]
    every = [0] + farthest_first(facets)
    wanted, calls = [], []
    for c, (begin, end) in enumerate(chunks):
        count = (end - begin) * per_channel
        where = (begin * per_channel // VB, count // VB)
        if c:
            choices = [(count, None, every)]
        else:
            soon = (end - begin) * len(early) * rows
            choices = [(soon, True, early), (count - soon, False, every)]
        for listed_count, choice, steps in choices:
            wanted.append(where + (listed_count, choice))
            calls.append((c, listed_count, steps))
    lists = group_lists(
        block_facet.reshape(-1, VB),
        block_tile.reshape(-1, VB),
        wanted,
        (facets, rows, halves),
        target_count,
    )
    parts = []
    for c, (begin, end) in enumerate(chunks):
        pieces = deal_channels(voltages, facets, begin, end, lists[:1] if c else [])
        got = [pieces[0]]
        for s in farthest_first(facets):
            pairs = [(i, i ^ s) for i in range(facets)]
            got.append(lax.ppermute(pieces[s], "stn", pairs))
        parts.append(got)
    tables = tuple(jnp.asarray(t) for t in transform_tables())
    cells = None
    for listed, (c, listed_count, steps) in zip(lists, calls):
        begin, end = chunks[c]
        held = slice(begin * per_channel, end * per_channel)
        got = [parts[c][every.index(t)] for t in steps]
        last = tables if end == channels else None
        cells = grid_call(
            listed, listed_count, stations, steps, got, offsets[held], cells, last, target_count
        )

    row_count = FG // chan_count
    pieces = cells.reshape(facets * chan_count, row_count, 2 * FG)
    pieces = lax.all_to_all(pieces, ("stn", "chan"), split_axis=0, concat_axis=0, tiled=True)
    channels_all = all_channels * chan_count
    norm_factor = 1.0 / math.sqrt(channels_all * stations * stations * KT * KT / facets)
    u_real, u_imag = taps_transform(kernel_taps[0])
    v_real, v_imag = taps_transform(kernel_taps[1])
    first_row = lax.axis_index("chan") * row_count
    u_real = lax.dynamic_slice_in_dim(u_real, first_row, row_count)[:, None] * norm_factor
    u_imag = lax.dynamic_slice_in_dim(u_imag, first_row, row_count)[:, None] * norm_factor
    w_real = u_real * v_real[None, :] - u_imag * v_imag[None, :]
    w_imag = u_real * v_imag[None, :] + u_imag * v_real[None, :]
    of_real = jnp.stack([w_real, w_imag])
    of_imag = jnp.stack([-w_imag, w_real])

    image = jnp.sum(pieces.astype(F32), axis=0)
    return image[None, :, :FG] * of_real + image[None, :, FG:] * of_imag


def solution(mesh):
    placed = (
        P("stn", "chan", None),
        P("chan", "stn", None, None),
        P("chan", "stn", None),
        P("chan", "stn", None, None),
        P(),
    )
    return jax.shard_map(
        body, mesh=mesh, in_specs=placed, out_specs=P(None, ("stn", "chan"), None), check_vma=False
    )
```

```python
import functools
import math

import jax
import jax.numpy as jnp
import ml_dtypes
import numpy as np
from jax import lax
from jax.experimental import pallas as pl
from jax.experimental.pallas import tpu as pltpu
from jax.sharding import PartitionSpec as P

VB = 128
TILE = 32
KT = 8
TS = 4
TT = 16
OFFS = 25
FG = TS * TILE

GROUP = 4
UNROLL = 48
CHUNK_ENDS = (2, 4)

F32, BF16, I32 = jnp.float32, jnp.bfloat16, jnp.int32
LAST_BY_LAST = (((1,), (1,)), ((), ()))


def whole_block(shape):
    return pl.BlockSpec(shape, lambda i, *_: (0,) * len(shape))


def list_places(count, target_count):
    most = (count + target_count * (GROUP - 1)) // GROUP
    most = -(-most // UNROLL) * UNROLL
    block_rows = -(-most * GROUP // VB)
    group_rows = -(-most // VB)
    return block_rows, group_rows, -(-(block_rows + group_rows + 1) // 8) * 8


def late_steps(panels):
    return range((panels + 1) // 2, panels - 1)


def early_blocks(shape, ids, me):
    panels, rows, halves = shape
    in_channel = ids - jnp.floor(ids * (1.0 / (panels * rows * halves))) * (panels * rows * halves)
    station = jnp.floor(in_channel * (1.0 / halves))
    panel = jnp.floor(station * (1.0 / rows)).astype(I32)
    step = jnp.bitwise_xor(panel, me)
    late = late_steps(panels)
    held = jnp.logical_or(step < late.start, step >= late.stop)
    own = in_channel - station * halves == (me * rows // VB).astype(F32)
    return jnp.logical_and(own, held).astype(F32)


def list_chunk(first_row, rows, listed_count, choice, shape, target_count, refs):
    facet_ref, tile_ref, out_ref = refs
    count = rows * VB
    block_rows, group_rows, _ = list_places(listed_count, target_count)
    exact = functools.partial(
        jnp.dot, precision=lax.Precision.HIGHEST, preferred_element_type=F32
    )
    dot = functools.partial(jnp.dot, preferred_element_type=F32)
    iota = lambda shape, dim: lax.broadcasted_iota(I32, shape, dim).astype(F32)
    target_ids = iota((target_count, VB), 0)
    square = (VB, VB)
    before = (iota(square, 0) < iota(square, 1)).astype(BF16)
    ones = jnp.ones(square, BF16)
    ids = iota((1, VB), 1)

    members, positions = [], []
    counted = jnp.zeros((target_count, VB), F32)
    for q in range(rows):
        r = first_row + q
        targets = (facet_ref[r : r + 1, :] * TT + tile_ref[r : r + 1, :]).astype(F32)
        chosen = jnp.ones((1, VB), F32)
        if choice is not None:
            early = early_blocks(shape, ids + q * VB, lax.axis_index("stn"))
            chosen = early if choice else 1.0 - early
        member = (target_ids == targets).astype(F32) * chosen
        members.append((member, chosen))
        positions.append(counted + dot(member.astype(BF16), before))
        counted = counted + dot(member.astype(BF16), ones)
    groups = jnp.floor((counted + (GROUP - 1)) * (1.0 / GROUP))
    lower = iota((target_count, target_count), 0) > iota((target_count, target_count), 1)
    first_group = exact(lower.astype(F32), groups)

    row_ids = iota((block_rows, VB), 0)
    lane_ids = iota(square, 0)
    held = jnp.zeros((3 * block_rows, VB), F32)
    for q, ((member, chosen), position) in enumerate(zip(members, positions)):
        slots = jnp.sum(member * (first_group * GROUP + position), axis=0, keepdims=True)
        slot_rows = jnp.floor(slots * (1.0 / VB))
        in_row = (row_ids == slot_rows).astype(F32) * chosen
        in_lane = (lane_ids == slots - slot_rows * VB).astype(BF16)
        left = jnp.concatenate([in_row, in_row * ids, in_row * q], axis=0).astype(BF16)
        held = held + lax.dot_general(left, in_lane, LAST_BY_LAST, preferred_element_type=F32)
    taken, low, high = (held[k * block_rows : (k + 1) * block_rows] for k in range(3))
    listed = jnp.where(taken > 0.5, low + VB * high, count)

    out_ref[...] = jnp.zeros_like(out_ref)
    out_ref[0:block_rows, :] = listed.astype(I32)
    for r in range(group_rows):
        group_ids = iota((target_count, VB), 1) + r * VB
        named = jnp.sum((group_ids >= first_group).astype(F32), axis=0, keepdims=True) - 1.0
        out_ref[block_rows + r : block_rows + r + 1, :] = named.astype(I32)
    total = jnp.sum(groups, axis=0, keepdims=True)
    turns = jnp.floor((total + (UNROLL - 1)) * (1.0 / UNROLL))
    last = block_rows + group_rows
    out_ref[last : last + 1, :] = turns.astype(I32)


def group_lists(facet_ids, tile_ids, wanted, shape, target_count):
    def kernel(facet_ref, tile_ref, *out_refs):
        for (first_row, rows, count, choice), out_ref in zip(wanted, out_refs):
            refs = (facet_ref, tile_ref, out_ref)
            list_chunk(first_row, rows, count, choice, shape, target_count, refs)

    shapes = [(list_places(count, target_count)[2], VB) for _, _, count, _ in wanted]
    lists = pl.pallas_call(
        kernel,
        grid=(1,),
        in_specs=[whole_block(facet_ids.shape), whole_block(tile_ids.shape)],
        out_specs=[whole_block(shape) for shape in shapes],
        out_shape=[jax.ShapeDtypeStruct(shape, I32) for shape in shapes],
        compiler_params=pltpu.CompilerParams(vmem_limit_bytes=32 << 20),
    )(facet_ids, tile_ids)
    return [x.reshape(-1) for x in lists]


def two_halves(x):
    high = x.astype(BF16)
    return high, (x - high.astype(F32)).astype(BF16)


def halves_of(table_ref):
    return table_ref[0], table_ref[1]


def split_dot(left, right):
    dot = functools.partial(jnp.dot, preferred_element_type=F32)
    return dot(left[0], right[0]) + (dot(left[0], right[1]) + dot(left[1], right[0]))


def grid_kernel(steps, first, last, places, list_ref, *refs):
    refs = list(refs)
    listed, list_done = refs.pop(-2), refs.pop(-1)
    list_copy = pltpu.make_async_copy(list_ref, listed, list_done)
    list_copy.start()
    part_refs = [refs.pop(0) for _ in steps]
    offset_ref = refs.pop(0)
    before_ref = None if first else refs.pop(0)
    tables = (refs.pop(0), refs.pop(0)) if last else None
    out_ref, whole, du_rows, dv_rows, re_rows, im_rows = refs[:6]
    cells = refs[6] if last else out_ref

    me = lax.axis_index("stn")
    targets_at, turns_at = places[0] * VB, (places[0] + places[1]) * VB
    channels, rows, width = part_refs[0].shape
    stations = whole.shape[1]
    samples = width // 2
    halves = stations // VB
    blocks = offset_ref.shape[0]

    if first:
        cells[...] = jnp.zeros_like(cells)
    else:
        cells[...] = before_ref[...]

    offsets = offset_ref[...]
    du = (offsets * 1311) >> 15
    du_rows[0:blocks] = du.astype(F32)
    dv_rows[0:blocks] = (offsets - du * OFFS).astype(F32)
    no_row = jnp.zeros((8, VB), F32)
    for row_ref in (du_rows, dv_rows, re_rows, im_rows):
        row_ref[blocks:] = no_row

    if len(steps) * rows < stations:
        whole[...] = jnp.zeros_like(whole)
    for step, part in zip(steps, part_refs):
        start = pl.multiple_of(jnp.bitwise_xor(me, step) * rows, rows)
        for k in range(channels):
            whole[k, pl.ds(start, rows), :] = part[k]

    scale = 1.0 / math.sqrt(samples)
    diagonal = lax.broadcasted_iota(I32, (stations, stations), 0) == lax.broadcasted_iota(
        I32, (stations, stations), 1
    )
    for k in range(channels):
        x = whole[k]
        swapped = jnp.concatenate([x[:, samples:], -x[:, :samples]], axis=1)
        for row_ref, left in ((re_rows, x), (im_rows, swapped)):
            vis = lax.dot_general(left, x, LAST_BY_LAST, preferred_element_type=F32) * scale
            vis = jnp.where(diagonal, 0.0, vis).astype(BF16).astype(F32)
            for h in range(halves):
                row_ref[pl.ds(k * stations * halves + h, stations, stride=halves), :] = vis[
                    :, h * VB : (h + 1) * VB
                ]

    half = lax.broadcasted_iota(I32, (16, VB), 0).astype(F32)
    cell_ids = [(half + 16 * part).astype(BF16) for part in range(TILE // 16)]
    none = jnp.zeros((16, VB), BF16)
    ones = jnp.ones((16, VB), BF16)

    def spread(row_ref, n):
        return jnp.broadcast_to(row_ref[pl.ds(n, 1), :], (16, VB)).astype(BF16)

    def block_pair(n):
        du_n, dv_n = spread(du_rows, n), spread(dv_rows, n)
        re_n, im_n = spread(re_rows, n), spread(im_rows, n)
        along_u = [jnp.where(ids == du_n, ones, none) for ids in cell_ids]
        along_v = [jnp.where(ids == dv_n, re_n, none) for ids in cell_ids]
        along_v += [jnp.where(ids == dv_n, im_n, none) for ids in cell_ids]
        return jnp.concatenate(along_u, axis=0), jnp.concatenate(along_v, axis=0)

    list_copy.wait()

    def turn(index, carry):
        sums = []
        for q in range(UNROLL):
            g = index * UNROLL + q
            pairs = [block_pair(listed[g * GROUP + p]) for p in range(GROUP)]
            left = jnp.concatenate([a for a, b in pairs], axis=1)
            right = jnp.concatenate([b for a, b in pairs], axis=1)
            sums.append(
                (g, lax.dot_general(left, right, LAST_BY_LAST, preferred_element_type=F32))
            )
        for g, total in sums:
            cells[listed[targets_at + g]] += total
        return carry

    lax.fori_loop(0, listed[turns_at], turn, 0)

    if last:
        row_table, column_table = tables
        facets = cells.shape[0] // TT
        grid = jnp.concatenate(
            [
                jnp.concatenate(
                    [
                        cells[f * TT + tu * TS + tv]
                        for f in range(facets)
                        for tv in range(TS)
                    ],
                    axis=1,
                )
                for tu in range(TS)
            ],
            axis=0,
        )
        columns = split_dot(halves_of(row_table), two_halves(grid))
        both = jnp.concatenate(
            [
                jnp.concatenate(
                    [
                        columns[q * FG : (q + 1) * FG, f * 2 * FG : (f + 1) * 2 * FG]
                        for q in range(2)
                    ],
                    axis=1,
                )
                for f in range(facets)
            ],
            axis=0,
        )
        image = split_dot(two_halves(both), halves_of(column_table))
        out_ref[...] = image.astype(out_ref.dtype)


def step_order(panels, chunk):
    late = late_steps(panels)
    far, near = [panels - 1][: panels - 1], [s for s in range(1, panels - 1) if s not in late]
    return (near + far if chunk else far + near) + list(late)


def deal_kernel(begin, end, facets, voltage_ref, *refs):
    outs, wide = refs[-facets - 1 : -1], refs[-1]
    rows, all_channels, width = voltage_ref.shape
    channels = all_channels // facets
    lanes = wide.shape[0]
    for q in range(rows):
        row = voltage_ref[q].astype(F32)
        for t in range(lanes):
            wide[t, q * all_channels : (q + 1) * all_channels, :] = row[:, t * VB : (t + 1) * VB]
    for s in range(facets):
        first = jnp.bitwise_xor(lax.axis_index("stn"), s) * channels
        for k in range(begin, end):
            taken = [wide[t, pl.ds(first + k, rows, stride=all_channels), :] for t in range(lanes)]
            outs[s][k - begin] = jnp.concatenate(taken, axis=1).astype(BF16)


def deal_channels(voltages, facets, begin, end, after):
    rows, all_channels, width = voltages.shape
    shape = (end - begin, rows, width)
    return pl.pallas_call(
        functools.partial(deal_kernel, begin, end, facets),
        grid=(1,),
        in_specs=[whole_block(voltages.shape)] + [pl.BlockSpec(memory_space=pl.ANY)] * len(after),
        out_specs=[whole_block(shape)] * facets,
        scratch_shapes=[pltpu.VMEM((width // VB, rows * all_channels, VB), F32)],
        out_shape=[jax.ShapeDtypeStruct(shape, voltages.dtype)] * facets,
        compiler_params=pltpu.CompilerParams(vmem_limit_bytes=32 << 20),
    )(voltages, *after)


def grid_call(listed, listed_count, stations, steps, parts, offsets, before, tables, target_count):
    channels, rows, width = parts[0].shape
    blocks = offsets.shape[0]
    first, last = before is None, tables is not None
    operands = list(parts) + [offsets]
    if not first:
        operands.append(before)
    if last:
        operands += list(tables)
    cells = (target_count, TILE, 2 * TILE)
    scratch = [pltpu.VMEM((channels, stations, width), BF16)]
    scratch += [pltpu.VMEM((blocks + 8, VB), F32)] * 4
    if last:
        scratch.append(pltpu.VMEM(cells, F32))
        out = jax.ShapeDtypeStruct((target_count // TT * FG, 2 * FG), BF16)
    else:
        out = jax.ShapeDtypeStruct(cells, F32)
    scratch += [pltpu.SMEM(listed.shape, I32), pltpu.SemaphoreType.DMA]
    return pl.pallas_call(
        functools.partial(
            grid_kernel, steps, first, last, list_places(listed_count, target_count)
        ),
        grid=(1,),
        in_specs=[pl.BlockSpec(memory_space=pl.ANY)] + [whole_block(x.shape) for x in operands],
        out_specs=whole_block(out.shape),
        scratch_shapes=scratch,
        out_shape=out,
        compiler_params=pltpu.CompilerParams(vmem_limit_bytes=48 << 20),
    )(listed, *operands)


def split_table(table):
    high = table.astype(ml_dtypes.bfloat16)
    return high, (table - high.astype(np.float64)).astype(ml_dtypes.bfloat16)


def transform_tables():
    ids = np.arange(FG)
    angles = (ids[:, None] * ids[None, :] % FG) * (2.0 * math.pi / FG)
    cosine, sine = np.cos(angles), -np.sin(angles)
    row_table = np.concatenate([cosine, sine], axis=0)
    straight = np.concatenate([cosine, sine], axis=1).reshape(TS, 1, TILE, 2 * FG)
    turned = np.concatenate([-sine, cosine], axis=1).reshape(TS, 1, TILE, 2 * FG)
    real = np.concatenate([straight, turned], axis=1).reshape(2 * FG, 2 * FG)
    imag = np.concatenate([turned, -straight], axis=1).reshape(2 * FG, 2 * FG)
    column_table = np.concatenate([real, imag], axis=0)
    return tuple(np.stack(split_table(t)) for t in (row_table, column_table))


def taps_transform(taps_row):
    index_ids = jnp.arange(FG, dtype=I32)
    phases = index_ids[:, None] * jnp.arange(KT, dtype=I32)[None, :] % FG
    angles = phases.astype(F32) * (2.0 * math.pi / FG)
    taps = taps_row.astype(F32)[None, :]
    return jnp.sum(jnp.cos(angles) * taps, axis=1), -jnp.sum(jnp.sin(angles) * taps, axis=1)


def body(voltages, block_facet, block_tile, vis_offset, kernel_taps):
    facets = lax.axis_size("stn")
    chan_count = lax.axis_size("chan")
    rows, all_channels, width = voltages.shape
    channels = all_channels // facets
    stations = rows * facets
    blocks = vis_offset.shape[2]
    target_count = facets * TT

    ends = [channels * e // 4 for e in CHUNK_ENDS]
    chunks = list(zip([0] + ends[:-1], ends))
    per_channel = blocks // channels
    offsets = vis_offset.reshape(blocks, VB)
    halves = stations // VB
    late = late_steps(facets)
    wanted, calls = [], []
    for c, (begin, end) in enumerate(chunks):
        count = (end - begin) * per_channel
        where = (begin * per_channel // VB, count // VB)
        steps = [0] + step_order(facets, c)
        early = [t for t in steps if t not in late]
        soon = (end - begin) * len(early) * rows
        for listed_count, choice, taken in ((soon, True, early), (count - soon, False, steps)):
            wanted.append(where + (listed_count, choice))
            calls.append((c, listed_count, taken))
    lists = group_lists(
        block_facet.reshape(-1, VB),
        block_tile.reshape(-1, VB),
        wanted,
        (facets, rows, halves),
        target_count,
    )
    parts = []
    for c, (begin, end) in enumerate(chunks):
        pieces = deal_channels(voltages, facets, begin, end, lists[:1] if c else [])
        got = {0: pieces[0]}
        for s in step_order(facets, c):
            pairs = [(i, i ^ s) for i in range(facets)]
            got[s] = lax.ppermute(pieces[s], "stn", pairs)
        parts.append(got)
    tables = tuple(jnp.asarray(t) for t in transform_tables())
    cells = None
    for call, (listed, (c, listed_count, steps)) in enumerate(zip(lists, calls)):
        begin, end = chunks[c]
        held = slice(begin * per_channel, end * per_channel)
        got = [parts[c][t] for t in steps]
        last = tables if call == len(calls) - 1 else None
        cells = grid_call(
            listed, listed_count, stations, steps, got, offsets[held], cells, last, target_count
        )

    row_count = FG // chan_count
    pieces = cells.reshape(facets * chan_count, row_count, 2 * FG)
    pieces = lax.all_to_all(pieces, ("stn", "chan"), split_axis=0, concat_axis=0, tiled=True)
    channels_all = all_channels * chan_count
    norm_factor = 1.0 / math.sqrt(channels_all * stations * stations * KT * KT / facets)
    u_real, u_imag = taps_transform(kernel_taps[0])
    v_real, v_imag = taps_transform(kernel_taps[1])
    first_row = lax.axis_index("chan") * row_count
    u_real = lax.dynamic_slice_in_dim(u_real, first_row, row_count)[:, None] * norm_factor
    u_imag = lax.dynamic_slice_in_dim(u_imag, first_row, row_count)[:, None] * norm_factor
    w_real = u_real * v_real[None, :] - u_imag * v_imag[None, :]
    w_imag = u_real * v_imag[None, :] + u_imag * v_real[None, :]
    of_real = jnp.stack([w_real, w_imag])
    of_imag = jnp.stack([-w_imag, w_real])

    image = jnp.sum(pieces.astype(F32), axis=0)
    return image[None, :, :FG] * of_real + image[None, :, FG:] * of_imag


def solution(mesh):
    placed = (
        P("stn", "chan", None),
        P("chan", "stn", None, None),
        P("chan", "stn", None),
        P("chan", "stn", None, None),
        P(),
    )
    return jax.shard_map(
        body, mesh=mesh, in_specs=placed, out_specs=P(None, ("stn", "chan"), None), check_vma=False
    )
```

```python
import functools
import math

import jax
import jax.numpy as jnp
import ml_dtypes
import numpy as np
from jax import lax
from jax.experimental import pallas as pl
from jax.experimental.pallas import tpu as pltpu
from jax.sharding import PartitionSpec as P

VB = 128
TILE = 32
KT = 8
TS = 4
TT = 16
OFFS = 25
FG = TS * TILE

GROUP = 4
UNROLL = 64
CHUNK_ENDS = (2, 4)

F32, BF16, I32 = jnp.float32, jnp.bfloat16, jnp.int32
LAST_BY_LAST = (((1,), (1,)), ((), ()))


def whole_block(shape):
    return pl.BlockSpec(shape, lambda i, *_: (0,) * len(shape))


def list_places(count, target_count):
    most = (count + target_count * (GROUP - 1)) // GROUP
    most = -(-most // UNROLL) * UNROLL
    block_rows = -(-most * GROUP // VB)
    group_rows = -(-most // VB)
    return block_rows, group_rows, -(-(block_rows + group_rows + 1) // 8) * 8


def late_steps(panels):
    return range((panels + 1) // 2, panels - 1)


def early_blocks(shape, ids, me):
    panels, rows, halves = shape
    in_channel = ids - jnp.floor(ids * (1.0 / (panels * rows * halves))) * (panels * rows * halves)
    station = jnp.floor(in_channel * (1.0 / halves))
    panel = jnp.floor(station * (1.0 / rows)).astype(I32)
    step = jnp.bitwise_xor(panel, me)
    late = late_steps(panels)
    held = jnp.logical_or(step < late.start, step >= late.stop)
    own = in_channel - station * halves == (me * rows // VB).astype(F32)
    return jnp.logical_and(own, held).astype(F32)


def list_chunk(first_row, rows, listed_count, choice, shape, target_count, refs):
    facet_ref, tile_ref, out_ref = refs
    count = rows * VB
    block_rows, group_rows, _ = list_places(listed_count, target_count)
    exact = functools.partial(
        jnp.dot, precision=lax.Precision.HIGHEST, preferred_element_type=F32
    )
    dot = functools.partial(jnp.dot, preferred_element_type=F32)
    iota = lambda shape, dim: lax.broadcasted_iota(I32, shape, dim).astype(F32)
    target_ids = iota((target_count, VB), 0)
    square = (VB, VB)
    before = (iota(square, 0) < iota(square, 1)).astype(BF16)
    ones = jnp.ones(square, BF16)
    ids = iota((1, VB), 1)

    members, positions = [], []
    counted = jnp.zeros((target_count, VB), F32)
    for q in range(rows):
        r = first_row + q
        targets = (facet_ref[r : r + 1, :] * TT + tile_ref[r : r + 1, :]).astype(F32)
        chosen = jnp.ones((1, VB), F32)
        if choice is not None:
            early = early_blocks(shape, ids + q * VB, lax.axis_index("stn"))
            chosen = early if choice else 1.0 - early
        member = (target_ids == targets).astype(F32) * chosen
        members.append((member, chosen))
        positions.append(counted + dot(member.astype(BF16), before))
        counted = counted + dot(member.astype(BF16), ones)
    groups = jnp.floor((counted + (GROUP - 1)) * (1.0 / GROUP))
    lower = iota((target_count, target_count), 0) > iota((target_count, target_count), 1)
    first_group = exact(lower.astype(F32), groups)

    row_ids = iota((block_rows, VB), 0)
    lane_ids = iota(square, 0)
    held = jnp.zeros((3 * block_rows, VB), F32)
    for q, ((member, chosen), position) in enumerate(zip(members, positions)):
        slots = jnp.sum(member * (first_group * GROUP + position), axis=0, keepdims=True)
        slot_rows = jnp.floor(slots * (1.0 / VB))
        in_row = (row_ids == slot_rows).astype(F32) * chosen
        in_lane = (lane_ids == slots - slot_rows * VB).astype(BF16)
        left = jnp.concatenate([in_row, in_row * ids, in_row * q], axis=0).astype(BF16)
        held = held + lax.dot_general(left, in_lane, LAST_BY_LAST, preferred_element_type=F32)
    taken, low, high = (held[k * block_rows : (k + 1) * block_rows] for k in range(3))
    listed = jnp.where(taken > 0.5, low + VB * high, count)

    out_ref[...] = jnp.zeros_like(out_ref)
    out_ref[0:block_rows, :] = listed.astype(I32)
    for r in range(group_rows):
        group_ids = iota((target_count, VB), 1) + r * VB
        named = jnp.sum((group_ids >= first_group).astype(F32), axis=0, keepdims=True) - 1.0
        out_ref[block_rows + r : block_rows + r + 1, :] = named.astype(I32)
    total = jnp.sum(groups, axis=0, keepdims=True)
    turns = jnp.floor((total + (UNROLL - 1)) * (1.0 / UNROLL))
    last = block_rows + group_rows
    out_ref[last : last + 1, :] = turns.astype(I32)


def group_lists(facet_ids, tile_ids, wanted, shape, target_count):
    def kernel(facet_ref, tile_ref, *out_refs):
        for (first_row, rows, count, choice), out_ref in zip(wanted, out_refs):
            refs = (facet_ref, tile_ref, out_ref)
            list_chunk(first_row, rows, count, choice, shape, target_count, refs)

    shapes = [(list_places(count, target_count)[2], VB) for _, _, count, _ in wanted]
    lists = pl.pallas_call(
        kernel,
        grid=(1,),
        in_specs=[whole_block(facet_ids.shape), whole_block(tile_ids.shape)],
        out_specs=[whole_block(shape) for shape in shapes],
        out_shape=[jax.ShapeDtypeStruct(shape, I32) for shape in shapes],
        compiler_params=pltpu.CompilerParams(vmem_limit_bytes=32 << 20),
    )(facet_ids, tile_ids)
    return [x.reshape(-1) for x in lists]


def two_halves(x):
    high = x.astype(BF16)
    return high, (x - high.astype(F32)).astype(BF16)


def halves_of(table_ref):
    return table_ref[0], table_ref[1]


def split_dot(left, right):
    dot = functools.partial(jnp.dot, preferred_element_type=F32)
    return dot(left[0], right[0]) + (dot(left[0], right[1]) + dot(left[1], right[0]))


def grid_kernel(steps, first, last, places, list_ref, *refs):
    refs = list(refs)
    listed, list_done = refs.pop(-2), refs.pop(-1)
    list_copy = pltpu.make_async_copy(list_ref, listed, list_done)
    list_copy.start()
    part_refs = [refs.pop(0) for _ in steps]
    offset_ref = refs.pop(0)
    before_ref = None if first else refs.pop(0)
    tables = (refs.pop(0), refs.pop(0)) if last else None
    out_ref, whole, du_rows, dv_rows, re_rows, im_rows = refs[:6]
    cells = refs[6] if last else out_ref

    me = lax.axis_index("stn")
    targets_at, turns_at = places[0] * VB, (places[0] + places[1]) * VB
    channels, rows, width = part_refs[0].shape
    stations = whole.shape[1]
    samples = width // 2
    halves = stations // VB
    blocks = offset_ref.shape[0]

    if first:
        cells[...] = jnp.zeros_like(cells)
    else:
        cells[...] = before_ref[...]

    offsets = offset_ref[...]
    du = (offsets * 1311) >> 15
    du_rows[0:blocks] = du.astype(F32)
    dv_rows[0:blocks] = (offsets - du * OFFS).astype(F32)
    no_row = jnp.zeros((8, VB), F32)
    for row_ref in (du_rows, dv_rows, re_rows, im_rows):
        row_ref[blocks:] = no_row

    if len(steps) * rows < stations:
        whole[...] = jnp.zeros_like(whole)
    for step, part in zip(steps, part_refs):
        start = pl.multiple_of(jnp.bitwise_xor(me, step) * rows, rows)
        for k in range(channels):
            whole[k, pl.ds(start, rows), :] = part[k]

    scale = 1.0 / math.sqrt(samples)
    diagonal = lax.broadcasted_iota(I32, (stations, stations), 0) == lax.broadcasted_iota(
        I32, (stations, stations), 1
    )
    for k in range(channels):
        x = whole[k]
        swapped = jnp.concatenate([x[:, samples:], -x[:, :samples]], axis=1)
        for row_ref, left in ((re_rows, x), (im_rows, swapped)):
            vis = lax.dot_general(left, x, LAST_BY_LAST, preferred_element_type=F32) * scale
            vis = jnp.where(diagonal, 0.0, vis).astype(BF16).astype(F32)
            for h in range(halves):
                row_ref[pl.ds(k * stations * halves + h, stations, stride=halves), :] = vis[
                    :, h * VB : (h + 1) * VB
                ]

    half = lax.broadcasted_iota(I32, (16, VB), 0).astype(F32)
    cell_ids = [(half + 16 * part).astype(BF16) for part in range(TILE // 16)]
    none = jnp.zeros((16, VB), BF16)
    ones = jnp.ones((16, VB), BF16)

    def spread(row_ref, n):
        return jnp.broadcast_to(row_ref[pl.ds(n, 1), :], (16, VB)).astype(BF16)

    def block_pair(n):
        du_n, dv_n = spread(du_rows, n), spread(dv_rows, n)
        re_n, im_n = spread(re_rows, n), spread(im_rows, n)
        along_u = [jnp.where(ids == du_n, ones, none) for ids in cell_ids]
        along_v = [jnp.where(ids == dv_n, re_n, none) for ids in cell_ids]
        along_v += [jnp.where(ids == dv_n, im_n, none) for ids in cell_ids]
        return jnp.concatenate(along_u, axis=0), jnp.concatenate(along_v, axis=0)

    list_copy.wait()

    def turn(index, carry):
        sums = []
        for q in range(UNROLL):
            g = index * UNROLL + q
            pairs = [block_pair(listed[g * GROUP + p]) for p in range(GROUP)]
            left = jnp.concatenate([a for a, b in pairs], axis=1)
            right = jnp.concatenate([b for a, b in pairs], axis=1)
            sums.append(
                (g, lax.dot_general(left, right, LAST_BY_LAST, preferred_element_type=F32))
            )
        for g, total in sums:
            cells[listed[targets_at + g]] += total
        return carry

    lax.fori_loop(0, listed[turns_at], turn, 0)

    if last:
        row_table, column_table = tables
        facets = cells.shape[0] // TT
        grid = jnp.concatenate(
            [
                jnp.concatenate(
                    [
                        cells[f * TT + tu * TS + tv]
                        for f in range(facets)
                        for tv in range(TS)
                    ],
                    axis=1,
                )
                for tu in range(TS)
            ],
            axis=0,
        )
        columns = split_dot(halves_of(row_table), two_halves(grid))
        both = jnp.concatenate(
            [
                jnp.concatenate(
                    [
                        columns[q * FG : (q + 1) * FG, f * 2 * FG : (f + 1) * 2 * FG]
                        for q in range(2)
                    ],
                    axis=1,
                )
                for f in range(facets)
            ],
            axis=0,
        )
        image = split_dot(two_halves(both), halves_of(column_table))
        out_ref[...] = image.astype(out_ref.dtype)


def step_order(panels, chunk):
    late = late_steps(panels)
    far, near = [panels - 1][: panels - 1], [s for s in range(1, panels - 1) if s not in late]
    return (near + far if chunk else far + near) + list(late)


def deal_kernel(begin, end, facets, voltage_ref, *refs):
    outs, wide = refs[-facets - 1 : -1], refs[-1]
    rows, all_channels, width = voltage_ref.shape
    channels = all_channels // facets
    lanes = wide.shape[0]
    for q in range(rows):
        row = voltage_ref[q].astype(F32)
        for t in range(lanes):
            wide[t, q * all_channels : (q + 1) * all_channels, :] = row[:, t * VB : (t + 1) * VB]
    for s in range(facets):
        first = jnp.bitwise_xor(lax.axis_index("stn"), s) * channels
        for k in range(begin, end):
            taken = [wide[t, pl.ds(first + k, rows, stride=all_channels), :] for t in range(lanes)]
            outs[s][k - begin] = jnp.concatenate(taken, axis=1).astype(BF16)


def deal_channels(voltages, facets, begin, end, after):
    rows, all_channels, width = voltages.shape
    shape = (end - begin, rows, width)
    return pl.pallas_call(
        functools.partial(deal_kernel, begin, end, facets),
        grid=(1,),
        in_specs=[whole_block(voltages.shape)] + [pl.BlockSpec(memory_space=pl.ANY)] * len(after),
        out_specs=[whole_block(shape)] * facets,
        scratch_shapes=[pltpu.VMEM((width // VB, rows * all_channels, VB), F32)],
        out_shape=[jax.ShapeDtypeStruct(shape, voltages.dtype)] * facets,
        compiler_params=pltpu.CompilerParams(vmem_limit_bytes=32 << 20),
    )(voltages, *after)


def grid_call(listed, listed_count, stations, steps, parts, offsets, before, tables, target_count):
    channels, rows, width = parts[0].shape
    blocks = offsets.shape[0]
    first, last = before is None, tables is not None
    operands = list(parts) + [offsets]
    if not first:
        operands.append(before)
    if last:
        operands += list(tables)
    cells = (target_count, TILE, 2 * TILE)
    scratch = [pltpu.VMEM((channels, stations, width), BF16)]
    scratch += [pltpu.VMEM((blocks + 8, VB), F32)] * 4
    if last:
        scratch.append(pltpu.VMEM(cells, F32))
        out = jax.ShapeDtypeStruct((target_count // TT * FG, 2 * FG), BF16)
    else:
        out = jax.ShapeDtypeStruct(cells, F32)
    scratch += [pltpu.SMEM(listed.shape, I32), pltpu.SemaphoreType.DMA]
    return pl.pallas_call(
        functools.partial(
            grid_kernel, steps, first, last, list_places(listed_count, target_count)
        ),
        grid=(1,),
        in_specs=[pl.BlockSpec(memory_space=pl.ANY)] + [whole_block(x.shape) for x in operands],
        out_specs=whole_block(out.shape),
        scratch_shapes=scratch,
        out_shape=out,
        compiler_params=pltpu.CompilerParams(vmem_limit_bytes=48 << 20),
    )(listed, *operands)


def split_table(table):
    high = table.astype(ml_dtypes.bfloat16)
    return high, (table - high.astype(np.float64)).astype(ml_dtypes.bfloat16)


def transform_tables():
    ids = np.arange(FG)
    angles = (ids[:, None] * ids[None, :] % FG) * (2.0 * math.pi / FG)
    cosine, sine = np.cos(angles), -np.sin(angles)
    row_table = np.concatenate([cosine, sine], axis=0)
    straight = np.concatenate([cosine, sine], axis=1).reshape(TS, 1, TILE, 2 * FG)
    turned = np.concatenate([-sine, cosine], axis=1).reshape(TS, 1, TILE, 2 * FG)
    real = np.concatenate([straight, turned], axis=1).reshape(2 * FG, 2 * FG)
    imag = np.concatenate([turned, -straight], axis=1).reshape(2 * FG, 2 * FG)
    column_table = np.concatenate([real, imag], axis=0)
    return tuple(np.stack(split_table(t)) for t in (row_table, column_table))


def taps_transform(taps_row):
    index_ids = jnp.arange(FG, dtype=I32)
    phases = index_ids[:, None] * jnp.arange(KT, dtype=I32)[None, :] % FG
    angles = phases.astype(F32) * (2.0 * math.pi / FG)
    taps = taps_row.astype(F32)[None, :]
    return jnp.sum(jnp.cos(angles) * taps, axis=1), -jnp.sum(jnp.sin(angles) * taps, axis=1)


def body(voltages, block_facet, block_tile, vis_offset, kernel_taps):
    facets = lax.axis_size("stn")
    chan_count = lax.axis_size("chan")
    rows, all_channels, width = voltages.shape
    channels = all_channels // facets
    stations = rows * facets
    blocks = vis_offset.shape[2]
    target_count = facets * TT

    ends = [channels * e // 4 for e in CHUNK_ENDS]
    chunks = list(zip([0] + ends[:-1], ends))
    per_channel = blocks // channels
    offsets = vis_offset.reshape(blocks, VB)
    halves = stations // VB
    late = late_steps(facets)
    wanted, calls = [], []
    for c, (begin, end) in enumerate(chunks):
        count = (end - begin) * per_channel
        where = (begin * per_channel // VB, count // VB)
        steps = [0] + step_order(facets, c)
        early = [t for t in steps if t not in late]
        soon = (end - begin) * len(early) * rows
        for listed_count, choice, taken in ((soon, True, early), (count - soon, False, steps)):
            wanted.append(where + (listed_count, choice))
            calls.append((c, listed_count, taken))
    lists = group_lists(
        block_facet.reshape(-1, VB),
        block_tile.reshape(-1, VB),
        wanted,
        (facets, rows, halves),
        target_count,
    )
    parts = []
    for c, (begin, end) in enumerate(chunks):
        pieces = deal_channels(voltages, facets, begin, end, lists[:1] if c else [])
        got = {0: pieces[0]}
        for s in step_order(facets, c):
            pairs = [(i, i ^ s) for i in range(facets)]
            got[s] = lax.ppermute(pieces[s], "stn", pairs)
        parts.append(got)
    tables = tuple(jnp.asarray(t) for t in transform_tables())
    cells = None
    for call, (listed, (c, listed_count, steps)) in enumerate(zip(lists, calls)):
        begin, end = chunks[c]
        held = slice(begin * per_channel, end * per_channel)
        got = [parts[c][t] for t in steps]
        last = tables if call == len(calls) - 1 else None
        cells = grid_call(
            listed, listed_count, stations, steps, got, offsets[held], cells, last, target_count
        )

    row_count = FG // chan_count
    pieces = cells.reshape(facets * chan_count, row_count, 2 * FG)
    pieces = lax.all_to_all(pieces, ("stn", "chan"), split_axis=0, concat_axis=0, tiled=True)
    channels_all = all_channels * chan_count
    norm_factor = 1.0 / math.sqrt(channels_all * stations * stations * KT * KT / facets)
    u_real, u_imag = taps_transform(kernel_taps[0])
    v_real, v_imag = taps_transform(kernel_taps[1])
    first_row = lax.axis_index("chan") * row_count
    u_real = lax.dynamic_slice_in_dim(u_real, first_row, row_count)[:, None] * norm_factor
    u_imag = lax.dynamic_slice_in_dim(u_imag, first_row, row_count)[:, None] * norm_factor
    w_real = u_real * v_real[None, :] - u_imag * v_imag[None, :]
    w_imag = u_real * v_imag[None, :] + u_imag * v_real[None, :]
    of_real = jnp.stack([w_real, w_imag])
    of_imag = jnp.stack([-w_imag, w_real])

    image = jnp.sum(pieces.astype(F32), axis=0)
    return image[None, :, :FG] * of_real + image[None, :, FG:] * of_imag


def solution(mesh):
    placed = (
        P("stn", "chan", None),
        P("chan", "stn", None, None),
        P("chan", "stn", None),
        P("chan", "stn", None, None),
        P(),
    )
    return jax.shard_map(
        body, mesh=mesh, in_specs=placed, out_specs=P(None, ("stn", "chan"), None), check_vma=False
    )
```

```python
import functools
import math

import jax
import jax.numpy as jnp
import ml_dtypes
import numpy as np
from jax import lax
from jax.experimental import pallas as pl
from jax.experimental.pallas import tpu as pltpu
from jax.sharding import PartitionSpec as P

VB = 128
TILE = 32
KT = 8
TS = 4
TT = 16
OFFS = 25
FG = TS * TILE

GROUP = 4
UNROLL = 64
CHUNK_ENDS = (2, 4)

F32, BF16, I32 = jnp.float32, jnp.bfloat16, jnp.int32
LAST_BY_LAST = (((1,), (1,)), ((), ()))


def whole_block(shape):
    return pl.BlockSpec(shape, lambda i, *_: (0,) * len(shape))


def list_places(count, target_count):
    most = (count + target_count * (GROUP - 1)) // GROUP
    most = -(-most // UNROLL) * UNROLL
    block_rows = -(-most * GROUP // VB)
    group_rows = -(-most // VB)
    return block_rows, group_rows, -(-(block_rows + group_rows + 1) // 8) * 8


def late_steps(panels):
    return range((panels + 1) // 2, panels - 1)


def early_blocks(shape, ids, me):
    panels, rows, halves = shape
    in_channel = ids - jnp.floor(ids * (1.0 / (panels * rows * halves))) * (panels * rows * halves)
    station = jnp.floor(in_channel * (1.0 / halves))
    panel = jnp.floor(station * (1.0 / rows)).astype(I32)
    step = jnp.bitwise_xor(panel, me)
    late = late_steps(panels)
    held = jnp.logical_or(step < late.start, step >= late.stop)
    own = in_channel - station * halves == (me * rows // VB).astype(F32)
    return jnp.logical_and(own, held).astype(F32)


def list_chunk(first_row, rows, listed_count, choice, shape, target_count, refs):
    facet_ref, tile_ref, out_ref = refs
    count = rows * VB
    block_rows, group_rows, _ = list_places(listed_count, target_count)
    exact = functools.partial(
        jnp.dot, precision=lax.Precision.HIGHEST, preferred_element_type=F32
    )
    dot = functools.partial(jnp.dot, preferred_element_type=F32)
    iota = lambda shape, dim: lax.broadcasted_iota(I32, shape, dim).astype(F32)
    target_ids = iota((target_count, VB), 0)
    square = (VB, VB)
    before = (iota(square, 0) < iota(square, 1)).astype(BF16)
    ones = jnp.ones(square, BF16)
    ids = iota((1, VB), 1)

    members, positions = [], []
    counted = jnp.zeros((target_count, VB), F32)
    for q in range(rows):
        r = first_row + q
        targets = (facet_ref[r : r + 1, :] * TT + tile_ref[r : r + 1, :]).astype(F32)
        chosen = jnp.ones((1, VB), F32)
        if choice is not None:
            early = early_blocks(shape, ids + q * VB, lax.axis_index("stn"))
            chosen = early if choice else 1.0 - early
        member = (target_ids == targets).astype(F32) * chosen
        members.append((member, chosen))
        positions.append(counted + dot(member.astype(BF16), before))
        counted = counted + dot(member.astype(BF16), ones)
    groups = jnp.floor((counted + (GROUP - 1)) * (1.0 / GROUP))
    lower = iota((target_count, target_count), 0) > iota((target_count, target_count), 1)
    first_group = exact(lower.astype(F32), groups)

    row_ids = iota((block_rows, VB), 0)
    lane_ids = iota(square, 0)
    held = jnp.zeros((3 * block_rows, VB), F32)
    for q, ((member, chosen), position) in enumerate(zip(members, positions)):
        slots = jnp.sum(member * (first_group * GROUP + position), axis=0, keepdims=True)
        slot_rows = jnp.floor(slots * (1.0 / VB))
        in_row = (row_ids == slot_rows).astype(F32) * chosen
        in_lane = (lane_ids == slots - slot_rows * VB).astype(BF16)
        left = jnp.concatenate([in_row, in_row * ids, in_row * q], axis=0).astype(BF16)
        held = held + lax.dot_general(left, in_lane, LAST_BY_LAST, preferred_element_type=F32)
    taken, low, high = (held[k * block_rows : (k + 1) * block_rows] for k in range(3))
    listed = jnp.where(taken > 0.5, low + VB * high, count)

    out_ref[...] = jnp.zeros_like(out_ref)
    out_ref[0:block_rows, :] = listed.astype(I32)
    for r in range(group_rows):
        group_ids = iota((target_count, VB), 1) + r * VB
        named = jnp.sum((group_ids >= first_group).astype(F32), axis=0, keepdims=True) - 1.0
        out_ref[block_rows + r : block_rows + r + 1, :] = named.astype(I32)
    total = jnp.sum(groups, axis=0, keepdims=True)
    turns = jnp.floor((total + (UNROLL - 1)) * (1.0 / UNROLL))
    last = block_rows + group_rows
    out_ref[last : last + 1, :] = turns.astype(I32)


def group_lists(facet_ids, tile_ids, wanted, shape, target_count):
    def kernel(facet_ref, tile_ref, *out_refs):
        for (first_row, rows, count, choice), out_ref in zip(wanted, out_refs):
            refs = (facet_ref, tile_ref, out_ref)
            list_chunk(first_row, rows, count, choice, shape, target_count, refs)

    shapes = [(list_places(count, target_count)[2], VB) for _, _, count, _ in wanted]
    lists = pl.pallas_call(
        kernel,
        grid=(1,),
        in_specs=[whole_block(facet_ids.shape), whole_block(tile_ids.shape)],
        out_specs=[whole_block(shape) for shape in shapes],
        out_shape=[jax.ShapeDtypeStruct(shape, I32) for shape in shapes],
        compiler_params=pltpu.CompilerParams(vmem_limit_bytes=32 << 20),
    )(facet_ids, tile_ids)
    return [x.reshape(-1) for x in lists]


def two_halves(x):
    high = x.astype(BF16)
    return high, (x - high.astype(F32)).astype(BF16)


def halves_of(table_ref):
    return table_ref[0], table_ref[1]


def split_dot(left, right):
    dot = functools.partial(jnp.dot, preferred_element_type=F32)
    return dot(left[0], right[0]) + (dot(left[0], right[1]) + dot(left[1], right[0]))


def grid_kernel(steps, first, last, places, list_ref, *refs):
    refs = list(refs)
    listed, list_done = refs.pop(-2), refs.pop(-1)
    list_copy = pltpu.make_async_copy(list_ref, listed, list_done)
    list_copy.start()
    part_refs = [refs.pop(0) for _ in steps]
    offset_ref = refs.pop(0)
    before_ref = None if first else refs.pop(0)
    tables = (refs.pop(0), refs.pop(0)) if last else None
    out_ref, whole, du_rows, dv_rows, re_rows, im_rows = refs[:6]
    cells = refs[6] if last else out_ref

    me = lax.axis_index("stn")
    targets_at, turns_at = places[0] * VB, (places[0] + places[1]) * VB
    channels, rows, width = part_refs[0].shape
    stations = whole.shape[1]
    samples = width // 2
    halves = stations // VB
    blocks = offset_ref.shape[0]

    if first:
        cells[...] = jnp.zeros_like(cells)
    else:
        cells[...] = before_ref[...]

    offsets = offset_ref[...]
    du = (offsets * 1311) >> 15
    du_rows[0:blocks] = du.astype(F32)
    dv_rows[0:blocks] = (offsets - du * OFFS).astype(F32)
    no_row = jnp.zeros((8, VB), F32)
    for row_ref in (du_rows, dv_rows, re_rows, im_rows):
        row_ref[blocks:] = no_row

    if len(steps) * rows < stations:
        whole[...] = jnp.zeros_like(whole)
    for step, part in zip(steps, part_refs):
        start = pl.multiple_of(jnp.bitwise_xor(me, step) * rows, rows)
        for k in range(channels):
            whole[k, pl.ds(start, rows), :] = part[k]

    scale = 1.0 / math.sqrt(samples)
    diagonal = lax.broadcasted_iota(I32, (stations, stations), 0) == lax.broadcasted_iota(
        I32, (stations, stations), 1
    )
    for k in range(channels):
        x = whole[k]
        swapped = jnp.concatenate([x[:, samples:], -x[:, :samples]], axis=1)
        for row_ref, left in ((re_rows, x), (im_rows, swapped)):
            vis = lax.dot_general(left, x, LAST_BY_LAST, preferred_element_type=F32) * scale
            vis = jnp.where(diagonal, 0.0, vis).astype(BF16).astype(F32)
            for h in range(halves):
                row_ref[pl.ds(k * stations * halves + h, stations, stride=halves), :] = vis[
                    :, h * VB : (h + 1) * VB
                ]

    half = lax.broadcasted_iota(I32, (16, VB), 0).astype(F32)
    cell_ids = [(half + 16 * part).astype(BF16) for part in range(TILE // 16)]
    none = jnp.zeros((16, VB), BF16)
    ones = jnp.ones((16, VB), BF16)

    def spread(row_ref, n):
        return jnp.broadcast_to(row_ref[pl.ds(n, 1), :], (16, VB)).astype(BF16)

    def block_pair(n):
        du_n, dv_n = spread(du_rows, n), spread(dv_rows, n)
        re_n, im_n = spread(re_rows, n), spread(im_rows, n)
        along_u = [jnp.where(ids == du_n, ones, none) for ids in cell_ids]
        along_v = [jnp.where(ids == dv_n, re_n, none) for ids in cell_ids]
        along_v += [jnp.where(ids == dv_n, im_n, none) for ids in cell_ids]
        return jnp.concatenate(along_u, axis=0), jnp.concatenate(along_v, axis=0)

    list_copy.wait()

    def turn(index, carry):
        sums = []
        for q in range(UNROLL):
            g = index * UNROLL + q
            pairs = [block_pair(listed[g * GROUP + p]) for p in range(GROUP)]
            left = jnp.concatenate([a for a, b in pairs], axis=1)
            right = jnp.concatenate([b for a, b in pairs], axis=1)
            sums.append(
                (g, lax.dot_general(left, right, LAST_BY_LAST, preferred_element_type=F32))
            )
        for g, total in sums:
            cells[listed[targets_at + g]] += total
        return carry

    lax.fori_loop(0, listed[turns_at], turn, 0)

    if last:
        row_table, column_table = tables
        facets = cells.shape[0] // TT
        grid = jnp.concatenate(
            [
                jnp.concatenate(
                    [
                        cells[f * TT + tu * TS + tv]
                        for f in range(facets)
                        for tv in range(TS)
                    ],
                    axis=1,
                )
                for tu in range(TS)
            ],
            axis=0,
        )
        columns = split_dot(halves_of(row_table), two_halves(grid))
        both = jnp.concatenate(
            [
                jnp.concatenate(
                    [
                        columns[q * FG : (q + 1) * FG, f * 2 * FG : (f + 1) * 2 * FG]
                        for q in range(2)
                    ],
                    axis=1,
                )
                for f in range(facets)
            ],
            axis=0,
        )
        both = both.astype(BF16)
        image = sum(
            jnp.dot(both, half, preferred_element_type=F32) for half in halves_of(column_table)
        )
        out_ref[...] = image.astype(out_ref.dtype)


def step_order(panels, chunk):
    late = late_steps(panels)
    far, near = [panels - 1][: panels - 1], [s for s in range(1, panels - 1) if s not in late]
    return (near + far if chunk else far + near) + list(late)


def deal_kernel(begin, end, facets, voltage_ref, *refs):
    outs, wide = refs[-facets - 1 : -1], refs[-1]
    rows, all_channels, width = voltage_ref.shape
    channels = all_channels // facets
    lanes = wide.shape[0]
    for q in range(rows):
        row = voltage_ref[q].astype(F32)
        for t in range(lanes):
            wide[t, q * all_channels : (q + 1) * all_channels, :] = row[:, t * VB : (t + 1) * VB]
    for s in range(facets):
        first = jnp.bitwise_xor(lax.axis_index("stn"), s) * channels
        for k in range(begin, end):
            taken = [wide[t, pl.ds(first + k, rows, stride=all_channels), :] for t in range(lanes)]
            outs[s][k - begin] = jnp.concatenate(taken, axis=1).astype(BF16)


def deal_channels(voltages, facets, begin, end, after):
    rows, all_channels, width = voltages.shape
    shape = (end - begin, rows, width)
    return pl.pallas_call(
        functools.partial(deal_kernel, begin, end, facets),
        grid=(1,),
        in_specs=[whole_block(voltages.shape)] + [pl.BlockSpec(memory_space=pl.ANY)] * len(after),
        out_specs=[whole_block(shape)] * facets,
        scratch_shapes=[pltpu.VMEM((width // VB, rows * all_channels, VB), F32)],
        out_shape=[jax.ShapeDtypeStruct(shape, voltages.dtype)] * facets,
        compiler_params=pltpu.CompilerParams(vmem_limit_bytes=32 << 20),
    )(voltages, *after)


def grid_call(listed, listed_count, stations, steps, parts, offsets, before, tables, target_count):
    channels, rows, width = parts[0].shape
    blocks = offsets.shape[0]
    first, last = before is None, tables is not None
    operands = list(parts) + [offsets]
    if not first:
        operands.append(before)
    if last:
        operands += list(tables)
    cells = (target_count, TILE, 2 * TILE)
    scratch = [pltpu.VMEM((channels, stations, width), BF16)]
    scratch += [pltpu.VMEM((blocks + 8, VB), F32)] * 4
    if last:
        scratch.append(pltpu.VMEM(cells, F32))
        out = jax.ShapeDtypeStruct((target_count // TT * FG, 2 * FG), BF16)
    else:
        out = jax.ShapeDtypeStruct(cells, F32)
    scratch += [pltpu.SMEM(listed.shape, I32), pltpu.SemaphoreType.DMA]
    return pl.pallas_call(
        functools.partial(
            grid_kernel, steps, first, last, list_places(listed_count, target_count)
        ),
        grid=(1,),
        in_specs=[pl.BlockSpec(memory_space=pl.ANY)] + [whole_block(x.shape) for x in operands],
        out_specs=whole_block(out.shape),
        scratch_shapes=scratch,
        out_shape=out,
        compiler_params=pltpu.CompilerParams(vmem_limit_bytes=48 << 20),
    )(listed, *operands)


def split_table(table):
    high = table.astype(ml_dtypes.bfloat16)
    return high, (table - high.astype(np.float64)).astype(ml_dtypes.bfloat16)


def transform_tables():
    ids = np.arange(FG)
    angles = (ids[:, None] * ids[None, :] % FG) * (2.0 * math.pi / FG)
    cosine, sine = np.cos(angles), -np.sin(angles)
    row_table = np.concatenate([cosine, sine], axis=0)
    straight = np.concatenate([cosine, sine], axis=1).reshape(TS, 1, TILE, 2 * FG)
    turned = np.concatenate([-sine, cosine], axis=1).reshape(TS, 1, TILE, 2 * FG)
    real = np.concatenate([straight, turned], axis=1).reshape(2 * FG, 2 * FG)
    imag = np.concatenate([turned, -straight], axis=1).reshape(2 * FG, 2 * FG)
    column_table = np.concatenate([real, imag], axis=0)
    return tuple(np.stack(split_table(t)) for t in (row_table, column_table))


def taps_transform(taps_row):
    index_ids = jnp.arange(FG, dtype=I32)
    phases = index_ids[:, None] * jnp.arange(KT, dtype=I32)[None, :] % FG
    angles = phases.astype(F32) * (2.0 * math.pi / FG)
    taps = taps_row.astype(F32)[None, :]
    return jnp.sum(jnp.cos(angles) * taps, axis=1), -jnp.sum(jnp.sin(angles) * taps, axis=1)


def body(voltages, block_facet, block_tile, vis_offset, kernel_taps):
    facets = lax.axis_size("stn")
    chan_count = lax.axis_size("chan")
    rows, all_channels, width = voltages.shape
    channels = all_channels // facets
    stations = rows * facets
    blocks = vis_offset.shape[2]
    target_count = facets * TT

    ends = [channels * e // 4 for e in CHUNK_ENDS]
    chunks = list(zip([0] + ends[:-1], ends))
    per_channel = blocks // channels
    offsets = vis_offset.reshape(blocks, VB)
    halves = stations // VB
    late = late_steps(facets)
    wanted, calls = [], []
    for c, (begin, end) in enumerate(chunks):
        count = (end - begin) * per_channel
        where = (begin * per_channel // VB, count // VB)
        steps = [0] + step_order(facets, c)
        early = [t for t in steps if t not in late]
        soon = (end - begin) * len(early) * rows
        for listed_count, choice, taken in ((soon, True, early), (count - soon, False, steps)):
            wanted.append(where + (listed_count, choice))
            calls.append((c, listed_count, taken))
    lists = group_lists(
        block_facet.reshape(-1, VB),
        block_tile.reshape(-1, VB),
        wanted,
        (facets, rows, halves),
        target_count,
    )
    parts = []
    for c, (begin, end) in enumerate(chunks):
        pieces = deal_channels(voltages, facets, begin, end, lists[:1] if c else [])
        got = {0: pieces[0]}
        for s in step_order(facets, c):
            pairs = [(i, i ^ s) for i in range(facets)]
            got[s] = lax.ppermute(pieces[s], "stn", pairs)
        parts.append(got)
    tables = tuple(jnp.asarray(t) for t in transform_tables())
    cells = None
    for call, (listed, (c, listed_count, steps)) in enumerate(zip(lists, calls)):
        begin, end = chunks[c]
        held = slice(begin * per_channel, end * per_channel)
        got = [parts[c][t] for t in steps]
        last = tables if call == len(calls) - 1 else None
        cells = grid_call(
            listed, listed_count, stations, steps, got, offsets[held], cells, last, target_count
        )

    row_count = FG // chan_count
    pieces = cells.reshape(facets * chan_count, row_count, 2 * FG)
    pieces = lax.all_to_all(pieces, ("stn", "chan"), split_axis=0, concat_axis=0, tiled=True)
    channels_all = all_channels * chan_count
    norm_factor = 1.0 / math.sqrt(channels_all * stations * stations * KT * KT / facets)
    u_real, u_imag = taps_transform(kernel_taps[0])
    v_real, v_imag = taps_transform(kernel_taps[1])
    first_row = lax.axis_index("chan") * row_count
    u_real = lax.dynamic_slice_in_dim(u_real, first_row, row_count)[:, None] * norm_factor
    u_imag = lax.dynamic_slice_in_dim(u_imag, first_row, row_count)[:, None] * norm_factor
    w_real = u_real * v_real[None, :] - u_imag * v_imag[None, :]
    w_imag = u_real * v_imag[None, :] + u_imag * v_real[None, :]
    of_real = jnp.stack([w_real, w_imag])
    of_imag = jnp.stack([-w_imag, w_real])

    image = jnp.sum(pieces.astype(F32), axis=0)
    return image[None, :, :FG] * of_real + image[None, :, FG:] * of_imag


def solution(mesh):
    placed = (
        P("stn", "chan", None),
        P("chan", "stn", None, None),
        P("chan", "stn", None),
        P("chan", "stn", None, None),
        P(),
    )
    return jax.shard_map(
        body, mesh=mesh, in_specs=placed, out_specs=P(None, ("stn", "chan"), None), check_vma=False
    )
```
